256 devices in a mesh: ha: 16 (over y_lo, x, core), wa: 16 (over y_hi, z).
Axes of the slice: x: 4, y: 4 (y_hi: 2, y_lo: 2; y = y_hi * 2 + y_lo), z: 8, core: 2. Of those that a mesh axis runs over, the one named last changes fastest.
Arguments:
- query_tokens: bfloat16 [2, 128, 128, 1536], P(None, 'ha', 'wa'), may hold values from -20 to 20
- key_tokens: bfloat16 [2, 128, 128, 1536], P(None, 'ha', 'wa'), may hold values from -20 to 20
- value_tokens: bfloat16 [2, 128, 128, 1536], P(None, 'ha', 'wa'), may hold values from -6 to 6
- grad_output: bfloat16 [2, 128, 128, 1536], P(None, 'ha', 'wa'), may hold values from -6 to 6
- text_keys: bfloat16 [256, 1536], replicated, may hold values from -6 to 6
- text_values: bfloat16 [256, 1536], replicated, may hold values from -6 to 6
- reach_tiles: int32 [12, 2], replicated, may hold values from 0 to 1, as said below
- text_count: int32 [1], replicated, may hold values from 128 to 256
- pad_mask: int32 [2, 128, 128], replicated, may hold values 0 or 1
Outputs:
- attn_output: bfloat16 [2, 128, 128, 1536], P(None, 'ha', 'wa')
- grad_query: bfloat16 [2, 128, 128, 1536], P(None, 'ha', 'wa')
- grad_key: bfloat16 [2, 128, 128, 1536], P(None, 'ha', 'wa')
- grad_value: bfloat16 [2, 128, 128, 1536], P(None, 'ha', 'wa')
- grad_text_key: bfloat16 [256, 1536], replicated
- grad_text_value: bfloat16 [256, 1536], replicated
The draws below stay inside these ranges and needn't reach their ends.
Inputs may be any that keep to these rules, and one draw needn't show every extreme that they name: `reach_tiles`: some head has reach 1 along the height tile index and some head reach 0 along the width tile index.
All inputs are finite; a program needn't handle non-finite values.
Results may differ from the reference program's by a relative error of at most 0.025.
Values may be sent and summed in bfloat16 or wider, within the bound.
A program may use at most 128 MiB of HBM per device.

```python
import jax
import jax.numpy as jnp
from jax import lax

HEADS = 12
HD = 128
TH = 8
TW = 8
TEXT = 256
FRAMES = 2
CH = 1536
NH = 128
NW = 128
N_HA = 16
N_WA = 16


def draw_query_tokens(key, part):
    key = jax.random.fold_in(key, 11)
    return jnp.clip(jax.random.normal(key, (FRAMES, NH, NW, HEADS * HD)), -4.0, 4.0).astype(jnp.bfloat16)


def draw_key_tokens(key, part):
    key = jax.random.fold_in(key, 12)
    return jnp.clip(jax.random.normal(key, (FRAMES, NH, NW, HEADS * HD)), -4.0, 4.0).astype(jnp.bfloat16)


def draw_reach_tiles(key, part):
    key = jax.random.fold_in(key, 21)
    first, second = jax.random.split(key)
    reach = jax.random.randint(first, (HEADS, 2), 0, 2)
    chosen = jax.random.randint(second, (), 0, HEADS)
    reach = reach.at[chosen, 0].set(1)
    reach = reach.at[(chosen + 1) % HEADS, 1].set(0)
    return reach.astype(jnp.int32)


def place_ends(drawn, stream_key, smallest, high):
    place = [jax.random.randint(jax.random.fold_in(stream_key, axis), (), 0, length) for axis, length in enumerate(drawn.shape)]
    longest = drawn.shape.index(max(drawn.shape))
    neighbour = place[:longest] + [(place[longest] + 1) % drawn.shape[longest]] + place[longest + 1:]
    return drawn.at[tuple(place)].set(smallest).at[tuple(neighbour)].set(high)


def level_of(key, dims, pieces, smallest, largest):
    factor_of, own = 1.0, jax.random.fold_in(key, 6)
    for position, shards_of in pieces:
        steps = jnp.exp(jax.random.uniform(jax.random.fold_in(own, position), (shards_of,), jnp.float32, smallest / len(pieces), largest / len(pieces)))
        factor_of = factor_of * jnp.repeat(steps, dims[position] // shards_of).reshape([-1 if axis == position else 1 for axis in range(len(dims))])
    return factor_of


def noise(stream_key, dims, deviation, bound, cuts=(), kind=jnp.bfloat16):
    values = jax.random.normal(stream_key, dims, jnp.float32) * deviation
    if len(cuts) > 0:
        values = level_of(stream_key, dims, cuts, -0.22, 0.18) * values
    return jnp.clip(values, min=-bound, max=bound).astype(kind)


def setup_inputs(seed: int = 0) -> dict:
    arg_keys = jax.random.split(jax.random.key(seed), 10)
    query_tokens = draw_query_tokens(jax.random.fold_in(arg_keys[9], 71), 0)
    key_tokens = draw_key_tokens(jax.random.fold_in(arg_keys[9], 71), 0)
    value_tokens = noise(arg_keys[2], (FRAMES, NH, NW, CH), 1.0, 6.0, ((1, 16), (2, 16)))
    grad_output = noise(arg_keys[3], (FRAMES, NH, NW, CH), 1.0, 6.0, ((1, 16), (2, 16)))
    text_keys = noise(arg_keys[4], (TEXT, CH), 1.0, 6.0)
    text_values = noise(arg_keys[5], (TEXT, CH), 1.0, 6.0)
    reach_tiles = draw_reach_tiles(jax.random.fold_in(arg_keys[9], 71), 0)
    text_count = jax.random.randint(arg_keys[7], (1,), TEXT // 2, TEXT + 1).astype(jnp.int32)
    pad_mask = place_ends((jax.random.randint(arg_keys[8], (FRAMES, NH, NW), 0, 8) < 7).astype(jnp.int32), jax.random.fold_in(arg_keys[8], 1), 0, 1)
    return dict(query_tokens=query_tokens, key_tokens=key_tokens, value_tokens=value_tokens, grad_output=grad_output, text_keys=text_keys, text_values=text_values, reach_tiles=reach_tiles, text_count=text_count, pad_mask=pad_mask)


def split_heads(tokens):
    return tokens.reshape(-1, HEADS, HD)


def inner_product(form, left, right):
    left, right = lax.optimization_barrier((left, right))
    return jnp.einsum(form, left.astype(jnp.float32), right.astype(jnp.float32))


def tile_offsets(frames):
    row_tiles = jnp.arange(3 * TH, dtype=jnp.int32) // TH - 1
    col_tiles = jnp.arange(3 * TW, dtype=jnp.int32) // TW - 1
    row_off = jnp.broadcast_to(row_tiles[None, :, None], (frames, 3 * TH, 3 * TW)).reshape(-1)
    col_off = jnp.broadcast_to(col_tiles[None, None, :], (frames, 3 * TH, 3 * TW)).reshape(-1)
    return row_off, col_off


def window(reach_tiles, row_off, col_off):
    return (jnp.abs(row_off)[None, :] <= reach_tiles[:, 0:1]) & (jnp.abs(col_off)[None, :] <= reach_tiles[:, 1:2])


def attend(query_by_head, extended_keys, extended_values, key_allowed, text_key_rows, text_value_rows, text_allowed):
    softmax_scale = HD ** -0.5
    video_scores = softmax_scale * inner_product('cfp,qfp->fcq', query_by_head, extended_keys)
    score_text = softmax_scale * inner_product('nhd,jhd->hnj', query_by_head, text_key_rows)
    video_scores = jnp.where(key_allowed[:, None, :], video_scores, -jnp.inf)
    score_text = jnp.where(text_allowed[None, None, :], score_text, -jnp.inf)
    highest = jnp.maximum(jnp.max(video_scores, axis=-1), jnp.max(score_text, axis=-1))
    summed = jnp.sum(jnp.exp(video_scores - highest[..., None]), axis=-1) + jnp.sum(jnp.exp(score_text - highest[..., None]), axis=-1)
    log_total = highest + jnp.log(summed)
    video_probability = jnp.exp(video_scores - log_total[..., None])
    prob_text = jnp.exp(score_text - log_total[..., None])
    video_rounded_scores = video_probability.astype(jnp.bfloat16)
    text_rounded_scores = prob_text.astype(jnp.bfloat16)
    attention_by_head = (inner_product('uzp,pux->zux', video_rounded_scores, extended_values) + inner_product('tsm,mtl->stl', text_rounded_scores, text_value_rows)).astype(jnp.bfloat16)
    return attention_by_head, log_total, video_probability, prob_text, text_rounded_scores


def backward_queries(query_by_head, gradient_by_head, attention_by_head, extended_keys, extended_values, text_key_rows, text_value_rows, video_probability, prob_text, text_rounded_scores):
    softmax_scale = HD ** -0.5
    attn_wide = lax.optimization_barrier(attention_by_head).astype(jnp.float32)
    row_delta_terms = jnp.sum(gradient_by_head.astype(jnp.float32) * attn_wide, axis=-1).T
    video_slope_terms = (video_probability * (inner_product('cfp,qfp->fcq', gradient_by_head, extended_values) - row_delta_terms[..., None])).astype(jnp.bfloat16)
    text_slope_terms = (prob_text * (inner_product('nhd,jhd->hnj', gradient_by_head, text_value_rows) - row_delta_terms[..., None])).astype(jnp.bfloat16)
    query_gradient = (softmax_scale * (inner_product('uzp,pux->zux', video_slope_terms, extended_keys) + inner_product('tsm,mtl->stl', text_slope_terms, text_key_rows))).astype(jnp.bfloat16)
    text_dk = softmax_scale * inner_product('hnj,nhd->jhd', text_slope_terms, query_by_head)
    text_dv = inner_product('hnj,nhd->jhd', text_rounded_scores, gradient_by_head)
    return query_gradient, row_delta_terms, video_slope_terms, text_dk, text_dv


def owner_grads(extended_queries, extended_gradient, log_ext, delta_ext, local_key_block, local_value_block, allowed):
    softmax_scale = HD ** -0.5
    logit_scores = softmax_scale * inner_product('yzo,azo->zya', extended_queries, local_key_block)
    probabilities = jnp.exp(jnp.where(allowed, logit_scores - log_ext[..., None], -jnp.inf))
    probability_gradient = inner_product('yzo,azo->zya', extended_gradient, local_value_block)
    slope_terms = (probabilities * (probability_gradient - delta_ext[..., None])).astype(jnp.bfloat16)
    key_gradient = (softmax_scale * inner_product('vtj,tvk->jvk', slope_terms, extended_queries)).astype(jnp.bfloat16)
    value_gradient = inner_product('vtj,tvk->jvk', probabilities.astype(jnp.bfloat16), extended_gradient).astype(jnp.bfloat16)
    return key_gradient, value_gradient


def reference(query_tokens, key_tokens, value_tokens, grad_output, text_keys, text_values, reach_tiles, text_count, pad_mask):
    frames = query_tokens.shape[0]
    channels = HEADS * HD
    text_allowed = jnp.arange(TEXT, dtype=jnp.int32) < text_count[0]
    row_off, col_off = tile_offsets(frames)
    inside = window(reach_tiles, row_off, col_off)
    margins = ((0, 0), (TH, TH), (TW, TW), (0, 0))
    mask_grid = pad_mask[..., None]
    key_wide = jnp.pad(key_tokens, margins)
    value_wide = jnp.pad(value_tokens, margins)
    mask_wide = jnp.pad(mask_grid, margins)
    text_key_rows = split_heads(text_keys)
    text_value_rows = split_heads(text_values)
    anchor = jnp.zeros((), jnp.int32)

    def extend(grid, row_tile, col_tile):
        return lax.dynamic_slice(grid, (anchor, row_tile * TH, col_tile * TW, anchor), (frames, 3 * TH, 3 * TW, grid.shape[3]))

    def own_block(grid, row_tile, col_tile):
        return lax.dynamic_slice(grid, (anchor, row_tile * TH, col_tile * TW, anchor), (frames, TH, TW, grid.shape[3]))

    def assemble(stacked, depth):
        grid = stacked.reshape(N_HA, N_WA, frames, TH, TW, depth)
        return grid.transpose(2, 0, 3, 1, 4, 5).reshape(frames, N_HA * TH, N_WA * TW, depth)

    def first_pass(carry, tile):
        row_tile = tile // N_WA
        col_tile = tile % N_WA
        query_by_head = split_heads(own_block(query_tokens, row_tile, col_tile))
        gradient_by_head = split_heads(own_block(grad_output, row_tile, col_tile))
        extended_keys = split_heads(extend(key_wide, row_tile, col_tile))
        extended_values = split_heads(extend(value_wide, row_tile, col_tile))
        key_allowed = inside & (extend(mask_wide, row_tile, col_tile).reshape(-1) > 0)[None, :]
        attention_by_head, log_total, video_probability, prob_text, text_rounded_scores = attend(query_by_head, extended_keys, extended_values, key_allowed, text_key_rows, text_value_rows, text_allowed)
        query_gradient, row_delta_terms, video_slope_terms, text_dk, text_dv = backward_queries(query_by_head, gradient_by_head, attention_by_head, extended_keys, extended_values, text_key_rows, text_value_rows, video_probability, prob_text, text_rounded_scores)
        stats = jnp.concatenate([log_total.T, row_delta_terms.T], axis=1)
        return (carry[0] + text_dk, carry[1] + text_dv), (attention_by_head, query_gradient, stats)

    start = (jnp.zeros((TEXT, HEADS, HD), jnp.float32), jnp.zeros((TEXT, HEADS, HD), jnp.float32))
    tiles = jnp.arange(N_HA * N_WA, dtype=jnp.int32)
    (text_dk, text_dv), (attn_all, gradq_all, stats_all) = lax.scan(first_pass, start, tiles)
    stats_grid = assemble(stats_all, 2 * HEADS)
    query_wide = jnp.pad(query_tokens, margins)
    gradout_wide = jnp.pad(grad_output, margins)
    stats_wide = jnp.pad(stats_grid, margins)

    def second_pass(tile):
        row_tile = tile // N_WA
        col_tile = tile % N_WA
        extended_queries = split_heads(extend(query_wide, row_tile, col_tile))
        extended_gradient = split_heads(extend(gradout_wide, row_tile, col_tile))
        flat_stats = extend(stats_wide, row_tile, col_tile).reshape(-1, 2 * HEADS)
        row_ok = (row_tile + row_off >= 0) & (row_tile + row_off < N_HA)
        col_ok = (col_tile + col_off >= 0) & (col_tile + col_off < N_WA)
        own_mask = own_block(mask_grid, row_tile, col_tile).reshape(-1) > 0
        allowed = (inside & (row_ok & col_ok)[None, :])[:, :, None] & own_mask[None, None, :]
        local_key_block = split_heads(own_block(key_tokens, row_tile, col_tile))
        local_value_block = split_heads(own_block(value_tokens, row_tile, col_tile))
        return owner_grads(extended_queries, extended_gradient, flat_stats[:, :HEADS].T, flat_stats[:, HEADS:].T, local_key_block, local_value_block, allowed)

    gradk_all, gradv_all = lax.map(second_pass, tiles)
    return (assemble(attn_all, channels), assemble(gradq_all, channels), assemble(gradk_all, channels), assemble(gradv_all, channels), text_dk.reshape(TEXT, channels).astype(jnp.bfloat16), text_dv.reshape(TEXT, channels).astype(jnp.bfloat16))
```

```python
import functools
import math

import jax
import jax.numpy as jnp
from jax import lax
from jax.experimental import pallas as pl
from jax.experimental.pallas import tpu as pltpu
from jax.sharding import PartitionSpec as P

HEADS = 12
HD = 128
TH = 8
TW = 8
TOK = 128
TEXT = 256
VID = 9 * TOK
KEYS = VID + TEXT
CH = HEADS * HD
GROUPS = 3
PER = HEADS // GROUPS
ROWS = TEXT // 8
SCALE = HD**-0.5
SCALE2 = SCALE * math.log2(math.e)
BIG = 1e30
MESH = pl.DeviceIdType.MESH
F32 = jnp.float32
BF16 = jnp.bfloat16
OFFSETS = tuple((dr, dc) for dr in (-1, 0, 1) for dc in (-1, 0, 1))


def dot_nt(a, b):
    return lax.dot_general(a, b, (((1,), (1,)), ((), ())), preferred_element_type=F32)


def dot_nn(a, b):
    return lax.dot_general(a, b, (((1,), (0,)), ((), ())), preferred_element_type=F32)


def dot_tn(a, b):
    return lax.dot_general(a, b, (((0,), (0,)), ((), ())), preferred_element_type=F32)


def cols(head):
    return pl.ds(pl.multiple_of(head * HD, HD), HD)


class Copy:
    def __init__(self, sems, number, src, dst, device, sends=None, receives=None):
        self.copy = pltpu.make_async_remote_copy(
            src_ref=src,
            dst_ref=dst,
            send_sem=sems[0].at[number],
            recv_sem=sems[1].at[number],
            device_id=device,
            device_id_type=MESH,
        )
        self.sends = sends
        self.receives = receives

    def start(self):
        if self.sends is None:
            self.copy.start()
        else:
            pl.when(self.sends)(self.copy.start)

    def wait_recv(self):
        if self.receives is None:
            self.copy.wait_recv()
        else:
            pl.when(self.receives)(self.copy.wait_recv)

    def wait_send(self):
        if self.sends is None:
            self.copy.wait_send()
        else:
            pl.when(self.sends)(self.copy.wait_send)


def main_kernel(
    sizes,
    q_ref,
    k_ref,
    v_ref,
    d_ref,
    tk_ref,
    tv_ref,
    bias_ref,
    qbias_ref,
    pad_ref,
    attn_ref,
    gq_ref,
    gk_ref,
    gv_ref,
    text_ref,
    kv_sw,
    kv_sh,
    kv_sc,
    kv_rw,
    kv_rh,
    kv_rc,
    qd_sw,
    qd_sh,
    qd_sc,
    qd_rw,
    qd_rh,
    qd_rc,
    left_ext,
    right_ext,
    stat_acc,
    stat_ext,
    own_part,
    pair_src,
    pair_dst,
    a_src,
    a_dst,
    z_acc,
    z_src,
    z_dst,
    b_all,
    send_sems,
    recv_sems,
):
    m_w, m_h, m_c = sizes
    ha = lax.axis_index("ha")
    wa = lax.axis_index("wa")
    core = ha % 2
    x = (ha // 2) % 4
    y = (wa // 8) * 2 + ha // 8
    z = wa % 8

    def device(y_, x_, core_, z_):
        return ((y_ % 2) * 8 + x_ * 2 + core_, (y_ // 2) * 8 + z_)

    def a_partner(step):
        along = (core * x + (1 - core) * y + step) % 4
        return along, device(core * y + (1 - core) * along, core * along + (1 - core) * x, core, z)

    def b_partner(step):
        along = (core * y + (1 - core) * x + step) % 4
        return along, device(core * along + (1 - core) * y, core * x + (1 - core) * along, core, z)

    def z_partner(step):
        along = (z + step) % 8
        return along, device(y, x, core, along)

    a_me = core * x + (1 - core) * y
    b_me = core * y + (1 - core) * x
    pair = device(y, x, 1 - core, z)
    has = {-1: (ha > 0, wa > 0), 1: (ha < 15, wa < 15)}

    def exists(dr, dc):
        terms = [has[dr][0]] if dr else []
        terms += [has[dc][1]] if dc else []
        return functools.reduce(jnp.logical_and, terms)

    barrier = pltpu.get_barrier_semaphore()

    def greet(target):
        pl.semaphore_signal(barrier, inc=1, device_id=target, device_id_type=MESH)

    expected = jnp.int32(14)
    for dr, dc in OFFSETS:
        if dr or dc:
            there = exists(dr, dc)
            pl.when(there)(functools.partial(greet, (ha + dr, wa + dc)))
            expected = expected + there.astype(jnp.int32)
    for step in (1, 2, 3):
        greet(a_partner(step)[1])
        greet(b_partner(step)[1])
    for step in range(1, 8):
        greet(z_partner(step)[1])
    greet(pair)

    counter = [0]
    sems = (send_sems, recv_sems)

    def copy(src, dst, target, sends=None, receives=None):
        number = counter[0]
        counter[0] += 1
        return Copy(sems, number, src, dst, target, sends, receives)

    def pack(first, second, sw, sh):
        for index, ref in ((0, first), (1, second)):
            for i in range(m_w):
                sw[index * m_w + i] = ref[:, cols(i)]
            for i in range(m_h):
                sh[index * m_h + i] = ref[:, cols(i)]

    def pack_corners(rw, sc):
        for side in (0, 1):
            for index in (0, 1):
                for i in range(m_c):
                    sc[side, index * m_c + i] = rw[side, index * m_w + i]

    def blank(rw, rh, rc):
        for side, sign in ((0, -1), (1, 1)):

            @pl.when(jnp.logical_not(has[sign][1]))
            def _():
                rw[side] = jnp.zeros(rw.shape[1:], rw.dtype)

            @pl.when(jnp.logical_not(has[sign][0]))
            def _():
                rh[side] = jnp.zeros(rh.shape[1:], rh.dtype)
                rc[side] = jnp.zeros(rc.shape[1:], rc.dtype)

    def halo(sw, sh, sc, rw, rh, rc):
        along_w, along_h, corner = [], [], []
        for side, sign in ((0, 1), (1, -1)):
            to, source = has[sign], has[-sign]
            along_w.append(copy(sw, rw.at[side], (ha, wa + sign), to[1], source[1]))
            along_h.append(copy(sh, rh.at[side], (ha + sign, wa), to[0], source[0]))
            corner.append(copy(sc, rc.at[side], (ha + sign, wa), to[0], source[0]))
        return along_w, along_h, corner

    kv_w, kv_h, kv_c = halo(kv_sw, kv_sh, kv_sc, kv_rw, kv_rh, kv_rc)
    qd_w, qd_h, qd_c = halo(qd_sw, qd_sh, qd_sc, qd_rw, qd_rh, qd_rc)
    stat_copies = [
        copy(
            stat_ext.at[4],
            stat_ext.at[(1 - dr) * 3 + (1 - dc)],
            (ha + dr, wa + dc),
            exists(dr, dc),
            exists(-dr, -dc),
        )
        for dr, dc in OFFSETS
        if dr or dc
    ]

    pack(k_ref, v_ref, kv_sw, kv_sh)
    pl.semaphore_wait(barrier, expected)
    for c in kv_w + kv_h:
        c.start()
    pack(q_ref, d_ref, qd_sw, qd_sh)
    blank(kv_rw, kv_rh, kv_rc)
    blank(qd_rw, qd_rh, qd_rc)
    for dr, dc in OFFSETS:
        if dr or dc:

            @pl.when(jnp.logical_not(exists(dr, dc)))
            def _():
                stat_ext[(dr + 1) * 3 + dc + 1] = jnp.zeros((32, TOK), F32)

    def assemble(ext, own_ref, index, rw, rh, rc, head):
        w, h, c = head, head, head
        for tile, (dr, dc) in enumerate(OFFSETS):
            if dr == 0 and dc == 0:
                block = own_ref[:, cols(head)]
            elif dr == 0:
                block = rw[(dc + 1) // 2, index * m_w + w]
            elif dc == 0:
                block = rh[(dr + 1) // 2, index * m_h + h]
            else:
                block = rc[(dr + 1) // 2, (dc + 1) // 2, index * m_c + c]
            ext[pl.ds(tile * TOK, TOK), :] = block

    lane = lax.broadcasted_iota(jnp.int32, (TOK, TOK), 1)

    def own_pass(head):
        assemble(left_ext, k_ref, 0, kv_rw, kv_rh, kv_rc, head)
        assemble(right_ext, v_ref, 1, kv_rw, kv_rh, kv_rc, head)
        left_ext[pl.ds(VID, TEXT), :] = tk_ref[:, cols(head)]
        right_ext[pl.ds(VID, TEXT), :] = tv_ref[:, cols(head)]
        query, grad = q_ref[:, cols(head)], d_ref[:, cols(head)]
        scores = dot_nt(query, left_ext[...]) * SCALE2 + bias_ref[pl.ds(head, 1), :]
        highest = jnp.max(scores, axis=1, keepdims=True)
        powers = jnp.exp2(scores - highest)
        total = jnp.sum(powers, axis=1, keepdims=True)
        probs = powers * (1.0 / total)
        probs_b = probs.astype(BF16)
        attn = dot_nn(probs_b, right_ext[...]).astype(BF16)
        attn_ref[:, cols(head)] = attn
        delta = jnp.sum(grad.astype(F32) * attn.astype(F32), axis=1, keepdims=True)
        slopes = (probs * (dot_nt(grad, right_ext[...]) - delta)).astype(BF16)
        gq_ref[:, cols(head)] = (SCALE * dot_nn(slopes, left_ext[...])).astype(BF16)
        log_total = highest + jnp.log(total) * math.log2(math.e)
        stat_acc[...] = jnp.where(
            lane == head, log_total, jnp.where(lane == head + 16, delta, stat_acc[...])
        )
        text_k = SCALE * dot_tn(slopes[:, VID:], query)
        text_v = dot_tn(probs_b[:, VID:], grad)
        own_part[head] = jnp.where(core == 0, text_k, text_v)
        pair_src[head] = jnp.where(core == 0, text_v, text_k).astype(BF16)

    def owner_pass(head):
        assemble(left_ext, q_ref, 0, qd_rw, qd_rh, qd_rc, head)
        assemble(right_ext, d_ref, 1, qd_rw, qd_rh, qd_rc, head)
        log_total = jnp.concatenate([stat_ext[t, pl.ds(head, 1), :] for t in range(9)], axis=1)
        delta = jnp.concatenate([stat_ext[t, pl.ds(head + 16, 1), :] for t in range(9)], axis=1)
        shift = log_total + qbias_ref[pl.ds(head, 1), :]
        queries, grads = left_ext[pl.ds(0, VID), :], right_ext[pl.ds(0, VID), :]
        probs = jnp.exp2(dot_nt(k_ref[:, cols(head)], queries) * SCALE2 - shift)
        slopes = (probs * (dot_nt(v_ref[:, cols(head)], grads) - delta)).astype(BF16)
        real = pad_ref[...] > 0
        gk_ref[:, cols(head)] = jnp.where(real, SCALE * dot_nn(slopes, queries), 0.0).astype(BF16)
        gv_ref[:, cols(head)] = jnp.where(real, dot_nn(probs.astype(BF16), grads), 0.0).astype(BF16)

    started = []

    def stage_pair(g):
        span = pl.ds(g * PER, PER)
        made = [copy(pair_src.at[span], pair_dst.at[span], pair)]
        return made, None

    def prepare_a(g):
        for i in range(PER):
            own_part[g * PER + i] = own_part[g * PER + i] + pair_dst[g * PER + i].astype(F32)

        made = []
        for step in (1, 2, 3):
            along, target = a_partner(step)
            a_src[g, step - 1] = own_part[g * PER + along].astype(BF16)
            made.append(copy(a_src.at[g, step - 1], a_dst.at[g, step - 1], target))
        return made

    def prepare_z(g):
        z_acc[g] = (
            own_part[g * PER + a_me]
            + a_dst[g, 0].astype(F32)
            + a_dst[g, 1].astype(F32)
            + a_dst[g, 2].astype(F32)
        )
        z_src[g] = z_acc[g].astype(BF16)
        made = []
        for step in range(1, 8):
            along, target = z_partner(step)
            rows = pl.ds(pl.multiple_of(along * ROWS, ROWS), ROWS)
            made.append(copy(z_src.at[g, rows], z_dst.at[g, step - 1], target))
        return made

    def prepare_b(g):
        total = z_acc[g, pl.ds(pl.multiple_of(z * ROWS, ROWS), ROWS), :]
        for step in range(7):
            total = total + z_dst[g, step].astype(F32)
        b_all[g, b_me] = total.astype(BF16)
        return [
            copy(b_all.at[g, b_me], b_all.at[g, b_me], b_partner(step)[1]) for step in (1, 2, 3)
        ]

    def prepare_z_back(g):
        total = b_all[g, 0].astype(F32)
        for i in (1, 2, 3):
            total = total + b_all[g, i].astype(F32)
        rows = pl.ds(pl.multiple_of(z * ROWS, ROWS), ROWS)
        piece = text_ref.at[core, g * PER + a_me, rows]
        text_ref[core, g * PER + a_me, rows, :] = total.astype(BF16)
        return [copy(piece, piece, z_partner(step)[1]) for step in range(1, 8)]

    def prepare_a_back(g):
        piece = text_ref.at[core, g * PER + a_me]
        return [copy(piece, piece, a_partner(step)[1]) for step in (1, 2, 3)]

    def prepare_pair_back(g):
        piece = text_ref.at[core, pl.ds(g * PER, PER)]
        return [copy(piece, piece, pair)]

    stages = (
        lambda g: stage_pair(g)[0],
        prepare_a,
        prepare_z,
        prepare_b,
        prepare_z_back,
        prepare_a_back,
        prepare_pair_back,
        lambda g: [],
    )
    flying = [[] for _ in range(GROUPS)]
    level = [0] * GROUPS

    def advance(g):
        if level[g] >= len(stages):
            return
        for c in flying[g]:
            c.wait_recv()
        flying[g] = stages[level[g]](g)
        level[g] += 1
        for c in flying[g]:
            c.start()
        started.extend(flying[g])

    for c in kv_w:
        c.wait_recv()
    pack_corners(kv_rw, kv_sc)
    for c in kv_c + qd_w + qd_h:
        c.start()
    for c in kv_h + kv_c:
        c.wait_recv()

    stat_acc[...] = jnp.zeros((TOK, TOK), F32)
    for g in range(GROUPS):

        @pl.loop(g * PER, (g + 1) * PER)
        def _(head):
            own_pass(head)

        if g == GROUPS - 1:
            stat_ext[4] = jnp.transpose(stat_acc[...])[:32]
            for c in stat_copies:
                c.start()
        for earlier in range(g + 1):
            advance(earlier)
        if g == 0:
            for c in qd_w:
                c.wait_recv()
            pack_corners(qd_rw, qd_sc)
            for c in qd_c:
                c.start()

    for c in qd_h + qd_c + stat_copies:
        c.wait_recv()
    for part in range(6):
        for g in range(GROUPS):
            advance(g)

        @pl.loop(part * 2, part * 2 + 2)
        def _(head):
            owner_pass(head)

    for _ in stages:
        for g in range(GROUPS):
            advance(g)
    for c in kv_w + kv_h + kv_c + qd_w + qd_h + qd_c + stat_copies + started:
        c.wait_send()
    assert counter[0] == N_COPIES


N_COPIES = 20 + GROUPS * 25


def finish_kernel(attn, gq, gk, gv, text, o_attn, o_gq, o_gk, o_gv, o_tk, o_tv, sems):
    moves = [
        pltpu.make_async_copy(s, d, sems.at[i])
        for i, (s, d) in enumerate(((attn, o_attn), (gq, o_gq), (gk, o_gk), (gv, o_gv)))
    ]
    for side, out in ((0, o_tk), (1, o_tv)):
        for h in range(HEADS):
            moves.append(
                pltpu.make_async_copy(
                    text.at[side, h],
                    out.at[:, pl.ds(h * HD, HD)],
                    sems.at[4 + side * HEADS + h],
                )
            )
    for m in moves:
        m.start()
    for m in moves:
        m.wait()


def fused(sizes, operands):
    m_w, m_h, m_c = sizes
    vmem = pl.BlockSpec(memory_space=pltpu.VMEM)
    halo = [
        pltpu.VMEM((2 * m_w, TOK, HD), BF16),
        pltpu.VMEM((2 * m_h, TOK, HD), BF16),
        pltpu.VMEM((2, 2 * m_c, TOK, HD), BF16),
        pltpu.VMEM((2, 2 * m_w, TOK, HD), BF16),
        pltpu.VMEM((2, 2 * m_h, TOK, HD), BF16),
        pltpu.VMEM((2, 2, 2 * m_c, TOK, HD), BF16),
    ]
    token = jax.ShapeDtypeStruct((TOK, CH), BF16)
    return pl.pallas_call(
        functools.partial(main_kernel, sizes),
        out_shape=(
            token,
            token,
            token,
            token,
            jax.ShapeDtypeStruct((2, HEADS, TEXT, HD), BF16),
        ),
        in_specs=[vmem] * 9,
        out_specs=(vmem,) * 5,
        scratch_shapes=halo
        + halo
        + [
            pltpu.VMEM((KEYS, HD), BF16),
            pltpu.VMEM((KEYS, HD), BF16),
            pltpu.VMEM((TOK, TOK), F32),
            pltpu.VMEM((9, 32, TOK), F32),
            pltpu.VMEM((HEADS, TEXT, HD), F32),
            pltpu.VMEM((HEADS, TEXT, HD), BF16),
            pltpu.VMEM((HEADS, TEXT, HD), BF16),
            pltpu.VMEM((GROUPS, 3, TEXT, HD), BF16),
            pltpu.VMEM((GROUPS, 3, TEXT, HD), BF16),
            pltpu.VMEM((GROUPS, TEXT, HD), F32),
            pltpu.VMEM((GROUPS, TEXT, HD), BF16),
            pltpu.VMEM((GROUPS, 7, ROWS, HD), BF16),
            pltpu.VMEM((GROUPS, 4, ROWS, HD), BF16),
            pltpu.SemaphoreType.DMA((N_COPIES,)),
            pltpu.SemaphoreType.DMA((N_COPIES,)),
        ],
        compiler_params=pltpu.CompilerParams(
            collective_id=0, has_side_effects=True, vmem_limit_bytes=56 * 1024 * 1024
        ),
    )(*operands)


def finish(attn, gq, gk, gv, text):
    any_space = pl.BlockSpec(memory_space=pl.ANY)
    token = jax.ShapeDtypeStruct((TOK, CH), BF16)
    rows = jax.ShapeDtypeStruct((TEXT, CH), BF16)
    return pl.pallas_call(
        finish_kernel,
        out_shape=(token, token, token, token, rows, rows),
        in_specs=[any_space] * 5,
        out_specs=(any_space,) * 6,
        scratch_shapes=[pltpu.SemaphoreType.DMA((4 + 2 * HEADS,))],
    )(attn, gq, gk, gv, text)


def body(
    query_tokens,
    key_tokens,
    value_tokens,
    grad_output,
    text_keys,
    text_values,
    reach_tiles,
    text_count,
    pad_mask,
):
    frames = query_tokens.shape[0]
    ha = lax.axis_index("ha")
    wa = lax.axis_index("wa")
    dr = jnp.array([o[0] for o in OFFSETS], jnp.int32)
    dc = jnp.array([o[1] for o in OFFSETS], jnp.int32)
    inside = (jnp.abs(dr)[None] <= reach_tiles[:, 0:1]) & (jnp.abs(dc)[None] <= reach_tiles[:, 1:2])
    wide = jnp.pad(pad_mask, ((0, 0), (TH, TH), (TW, TW)))
    tiles = lax.dynamic_slice(wide, (0, ha * TH, wa * TW), (frames, 3 * TH, 3 * TW))
    tiles = tiles.reshape(frames, 3, TH, 3, TW).transpose(1, 3, 0, 2, 4).reshape(9, TOK)
    allowed = inside[:, :, None] & (tiles > 0)[None]
    live = jnp.broadcast_to(jnp.arange(TEXT, dtype=jnp.int32) < text_count[0], (HEADS, TEXT))
    bias = jnp.where(
        jnp.concatenate([allowed.reshape(HEADS, VID), live], axis=1), 0.0, -BIG
    ).astype(F32)
    there = (ha + dr >= 0) & (ha + dr < 16) & (wa + dc >= 0) & (wa + dc < 16)
    qbias = jnp.where(inside & there[None], 0.0, BIG).astype(F32)
    qbias = jnp.broadcast_to(qbias[:, :, None], (HEADS, 9, TOK)).reshape(HEADS, VID)
    pad = jnp.broadcast_to(tiles[4][:, None], (TOK, HD)).astype(F32)
    operands = [t.reshape(TOK, CH) for t in (query_tokens, key_tokens, value_tokens, grad_output)]
    operands += [text_keys, text_values, bias, qbias, pad]
    attn, gq, gk, gv, tk, tv = finish(*fused((HEADS, HEADS, HEADS), operands))
    shape = query_tokens.shape
    return (
        attn.reshape(shape),
        gq.reshape(shape),
        gk.reshape(shape),
        gv.reshape(shape),
        tk,
        tv,
    )


def solution(mesh):
    tokens = P(None, "ha", "wa", None)
    return jax.shard_map(
        body,
        mesh=mesh,
        in_specs=(tokens,) * 4 + (P(),) * 5,
        out_specs=(tokens,) * 4 + (P(), P()),
        check_vma=False,
    )
```

```python
import functools
import math

import jax
import jax.numpy as jnp
from jax import lax
from jax.experimental import pallas as pl
from jax.experimental.pallas import tpu as pltpu
from jax.sharding import PartitionSpec as P

HEADS = 12
HD = 128
TH = 8
TW = 8
TOK = 128
TEXT = 256
VID = 9 * TOK
KEYS = VID + TEXT
CH = HEADS * HD
GROUPS = 3
PER = HEADS // GROUPS
ROWS = TEXT // 8
SCALE = HD**-0.5
SCALE2 = SCALE * math.log2(math.e)
BIG = 1e30
MESH = pl.DeviceIdType.MESH
F32 = jnp.float32
BF16 = jnp.bfloat16
OFFSETS = tuple((dr, dc) for dr in (-1, 0, 1) for dc in (-1, 0, 1))


def dot_nt(a, b):
    return lax.dot_general(a, b, (((1,), (1,)), ((), ())), preferred_element_type=F32)


def dot_nn(a, b):
    return lax.dot_general(a, b, (((1,), (0,)), ((), ())), preferred_element_type=F32)


def dot_tn(a, b):
    return lax.dot_general(a, b, (((0,), (0,)), ((), ())), preferred_element_type=F32)


def cols(head):
    return pl.ds(pl.multiple_of(head * HD, HD), HD)


class Copy:
    def __init__(self, sems, number, src, dst, device, sends=None, receives=None):
        self.copy = pltpu.make_async_remote_copy(
            src_ref=src,
            dst_ref=dst,
            send_sem=sems[0].at[number],
            recv_sem=sems[1].at[number],
            device_id=device,
            device_id_type=MESH,
        )
        self.sends = sends
        self.receives = receives

    def start(self):
        if self.sends is None:
            self.copy.start()
        else:
            pl.when(self.sends)(self.copy.start)

    def wait_recv(self):
        if self.receives is None:
            self.copy.wait_recv()
        else:
            pl.when(self.receives)(self.copy.wait_recv)

    def wait_send(self):
        if self.sends is None:
            self.copy.wait_send()
        else:
            pl.when(self.sends)(self.copy.wait_send)


def regions(sizes):
    m_w, m_h = sizes
    c, b = HEADS - m_w, HEADS - m_h
    return (
        (range(0, c), (1, 4, 7)),
        (range(c, c + b), (3, 4, 5)),
        (range(c + b, HEADS), tuple(range(9))),
    )


def segments(sizes, step):
    runs = []
    for kind, (span, tiles) in enumerate(regions(sizes)):
        low = span.start
        while low < span.stop:
            high = min(span.stop, (low // step + 1) * step)
            runs.append((kind, low, high, tiles))
            low = high
    return runs


def main_kernel(
    sizes,
    kv_ref,
    qd_ref,
    text_in,
    bias_ref,
    qbias_ref,
    pad_ref,
    attn_ref,
    gq_ref,
    gk_ref,
    gv_ref,
    text_ref,
    kv_rw,
    kv_rh,
    kv_rc,
    qd_rw,
    qd_rh,
    qd_rc,
    left_ext,
    right_ext,
    stat_acc,
    stat_ext,
    own_part,
    pair_src,
    pair_dst,
    a_src,
    a_dst,
    z_acc,
    z_src,
    z_dst,
    b_all,
    send_sems,
    recv_sems,
):
    m_w, m_h = sizes
    n_c, n_b = HEADS - m_w, HEADS - m_h
    n_a = HEADS - n_c - n_b
    ha = lax.axis_index("ha")
    wa = lax.axis_index("wa")
    core = ha % 2
    x = (ha // 2) % 4
    y = (wa // 8) * 2 + ha // 8
    z = wa % 8

    def device(y_, x_, core_, z_):
        return ((y_ % 2) * 8 + x_ * 2 + core_, (y_ // 2) * 8 + z_)

    def a_partner(step):
        along = (core * x + (1 - core) * y + step) % 4
        return along, device(core * y + (1 - core) * along, core * along + (1 - core) * x, core, z)

    def b_partner(step):
        along = (core * y + (1 - core) * x + step) % 4
        return along, device(core * along + (1 - core) * y, core * x + (1 - core) * along, core, z)

    def z_partner(step):
        along = (z + step) % 8
        return along, device(y, x, core, along)

    a_me = core * x + (1 - core) * y
    b_me = core * y + (1 - core) * x
    pair = device(y, x, 1 - core, z)
    has = {-1: (ha > 0, wa > 0), 1: (ha < 15, wa < 15)}

    def exists(dr, dc):
        terms = [has[dr][0]] if dr else []
        terms += [has[dc][1]] if dc else []
        return functools.reduce(jnp.logical_and, terms)

    barrier = pltpu.get_barrier_semaphore()

    def greet(target):
        pl.semaphore_signal(barrier, inc=1, device_id=target, device_id_type=MESH)

    expected = jnp.int32(14)
    for dr, dc in OFFSETS:
        if dr or dc:
            there = exists(dr, dc)
            pl.when(there)(functools.partial(greet, (ha + dr, wa + dc)))
            expected = expected + there.astype(jnp.int32)
    for step in (1, 2, 3):
        greet(a_partner(step)[1])
        greet(b_partner(step)[1])
    for step in range(1, 8):
        greet(z_partner(step)[1])
    greet(pair)

    counter = [0]
    sems = (send_sems, recv_sems)

    def copy(src, dst, target, sends=None, receives=None):
        number = counter[0]
        counter[0] += 1
        return Copy(sems, number, src, dst, target, sends, receives)

    def blank(rw, rh, rc):
        for side, sign in ((0, -1), (1, 1)):

            @pl.when(jnp.logical_not(has[sign][1]))
            def _():
                rw[side] = jnp.zeros(rw.shape[1:], rw.dtype)

            @pl.when(jnp.logical_not(has[sign][0]))
            def _():
                rh[side] = jnp.zeros(rh.shape[1:], rh.dtype)
                rc[side] = jnp.zeros(rc.shape[1:], rc.dtype)

    def halo(own, rw, rh, rc):
        along_w, along_h, corner = [], [], []
        for side, sign in ((0, 1), (1, -1)):
            to, source = has[sign], has[-sign]
            along_w.append(
                copy(own.at[:, pl.ds(n_c, m_w)], rw.at[side], (ha, wa + sign), to[1], source[1])
            )
            for low, count, slot in ((0, n_c, 0), (n_c + n_b, n_a, n_c)):
                if count:
                    along_h.append(
                        copy(
                            own.at[:, pl.ds(low, count)],
                            rh.at[side, :, pl.ds(slot, count)],
                            (ha + sign, wa),
                            to[0],
                            source[0],
                        )
                    )
            corner.append(
                copy(rw.at[:, :, pl.ds(n_b, n_a)], rc.at[side], (ha + sign, wa), to[0], source[0])
            )
        return along_w, along_h, corner

    kv_w, kv_h, kv_c = halo(kv_ref, kv_rw, kv_rh, kv_rc)
    qd_w, qd_h, qd_c = halo(qd_ref, qd_rw, qd_rh, qd_rc)
    stat_copies = [
        copy(
            stat_ext.at[4],
            stat_ext.at[(1 - dr) * 3 + (1 - dc)],
            (ha + dr, wa + dc),
            exists(dr, dc),
            exists(-dr, -dc),
        )
        for dr, dc in OFFSETS
        if dr or dc
    ]

    pl.semaphore_wait(barrier, expected)
    for c in kv_h + kv_w:
        c.start()
    blank(kv_rw, kv_rh, kv_rc)
    blank(qd_rw, qd_rh, qd_rc)
    for dr, dc in OFFSETS:
        if dr or dc:

            @pl.when(jnp.logical_not(exists(dr, dc)))
            def _():
                stat_ext[(dr + 1) * 3 + dc + 1] = jnp.zeros((32, TOK), F32)

    def block(own_ref, index, rw, rh, rc, kind, position, tile):
        dr, dc = OFFSETS[tile]
        if dr == 0 and dc == 0:
            return own_ref[index, position]
        if dr == 0:
            return rw[(dc + 1) // 2, index, position - n_c]
        if dc == 0:
            return rh[(dr + 1) // 2, index, position if kind == 0 else position - n_b]
        return rc[(dr + 1) // 2, (dc + 1) // 2, index, position - n_c - n_b]

    def assemble(ext, first, own_ref, index, rw, rh, rc, kind, position, tiles):
        for i, tile in enumerate(tiles):
            ext[pl.ds(first + i * TOK, TOK), :] = block(
                own_ref, index, rw, rh, rc, kind, position, tile
            )

    lane = lax.broadcasted_iota(jnp.int32, (TOK, TOK), 1)

    def own_pass(kind, tiles, p):
        kv_halo = (kv_rw, kv_rh, kv_rc, kind, p, tiles)
        left_ext[pl.ds(0, TEXT), :] = text_in[0, p]
        right_ext[pl.ds(0, TEXT), :] = text_in[1, p]
        assemble(left_ext, TEXT, kv_ref, 0, *kv_halo)
        assemble(right_ext, TEXT, kv_ref, 1, *kv_halo)
        keys = left_ext[pl.ds(0, TEXT + len(tiles) * TOK), :]
        values = right_ext[pl.ds(0, TEXT + len(tiles) * TOK), :]
        query, grad = qd_ref[0, p], qd_ref[1, p]
        bias = jnp.concatenate([bias_ref[p, pl.ds(t, 1), :] for t in (9, 10) + tiles], axis=1)
        scores = dot_nt(query, keys) * SCALE2 + bias
        highest = jnp.max(scores, axis=1, keepdims=True)
        powers = jnp.exp2(scores - highest)
        total = jnp.sum(powers, axis=1, keepdims=True)
        probs = powers * (1.0 / total)
        probs_b = probs.astype(BF16)
        attn = dot_nn(probs_b, values).astype(BF16)
        attn_ref[p] = attn
        delta = jnp.sum(grad.astype(F32) * attn.astype(F32), axis=1, keepdims=True)
        slopes = (probs * (dot_nt(grad, values) - delta)).astype(BF16)
        gq_ref[p] = (SCALE * dot_nn(slopes, keys)).astype(BF16)
        log_total = highest + jnp.log(total) * math.log2(math.e)
        stat_acc[...] = jnp.where(
            lane == p, log_total, jnp.where(lane == p + 16, delta, stat_acc[...])
        )
        text_k = SCALE * dot_tn(slopes[:, :TEXT], query)
        text_v = dot_tn(probs_b[:, :TEXT], grad)
        own_part[p] = jnp.where(core == 0, text_k, text_v)
        pair_src[p] = jnp.where(core == 0, text_v, text_k).astype(BF16)

    def owner_pass(kind, tiles, p):
        qd_halo = (qd_rw, qd_rh, qd_rc, kind, p, tiles)
        assemble(left_ext, 0, qd_ref, 0, *qd_halo)
        assemble(right_ext, 0, qd_ref, 1, *qd_halo)
        log_total = jnp.concatenate(
            [stat_ext[t, pl.ds(p, 1), :] + qbias_ref[p, pl.ds(t, 1), :] for t in tiles], axis=1
        )
        delta = jnp.concatenate([stat_ext[t, pl.ds(p + 16, 1), :] for t in tiles], axis=1)
        queries = left_ext[pl.ds(0, len(tiles) * TOK), :]
        grads = right_ext[pl.ds(0, len(tiles) * TOK), :]
        probs = jnp.exp2(dot_nt(kv_ref[0, p], queries) * SCALE2 - log_total)
        slopes = (probs * (dot_nt(kv_ref[1, p], grads) - delta)).astype(BF16)
        real = pad_ref[...] > 0
        gk_ref[p] = jnp.where(real, SCALE * dot_nn(slopes, queries), 0.0).astype(BF16)
        gv_ref[p] = jnp.where(real, dot_nn(probs.astype(BF16), grads), 0.0).astype(BF16)

    started = []

    def stage_pair(g):
        span = pl.ds(g * PER, PER)
        made = [copy(pair_src.at[span], pair_dst.at[span], pair)]
        return made, None

    def prepare_a(g):
        for i in range(PER):
            own_part[g * PER + i] = own_part[g * PER + i] + pair_dst[g * PER + i].astype(F32)

        made = []
        for step in (1, 2, 3):
            along, target = a_partner(step)
            a_src[g, step - 1] = own_part[g * PER + along].astype(BF16)
            made.append(copy(a_src.at[g, step - 1], a_dst.at[g, step - 1], target))
        return made

    def prepare_z(g):
        z_acc[g] = (
            own_part[g * PER + a_me]
            + a_dst[g, 0].astype(F32)
            + a_dst[g, 1].astype(F32)
            + a_dst[g, 2].astype(F32)
        )
        z_src[g] = z_acc[g].astype(BF16)
        made = []
        for step in range(1, 8):
            along, target = z_partner(step)
            rows = pl.ds(pl.multiple_of(along * ROWS, ROWS), ROWS)
            made.append(copy(z_src.at[g, rows], z_dst.at[g, step - 1], target))
        return made

    def prepare_b(g):
        total = z_acc[g, pl.ds(pl.multiple_of(z * ROWS, ROWS), ROWS), :]
        for step in range(7):
            total = total + z_dst[g, step].astype(F32)
        b_all[g, b_me] = total.astype(BF16)
        return [
            copy(b_all.at[g, b_me], b_all.at[g, b_me], b_partner(step)[1]) for step in (1, 2, 3)
        ]

    def prepare_z_back(g):
        total = b_all[g, 0].astype(F32)
        for i in (1, 2, 3):
            total = total + b_all[g, i].astype(F32)
        rows = pl.ds(pl.multiple_of(z * ROWS, ROWS), ROWS)
        piece = text_ref.at[core, g * PER + a_me, rows]
        text_ref[core, g * PER + a_me, rows, :] = total.astype(BF16)
        return [copy(piece, piece, z_partner(step)[1]) for step in range(1, 8)]

    def prepare_a_back(g):
        piece = text_ref.at[core, g * PER + a_me]
        return [copy(piece, piece, a_partner(step)[1]) for step in (1, 2, 3)]

    def prepare_pair_back(g):
        piece = text_ref.at[core, pl.ds(g * PER, PER)]
        return [copy(piece, piece, pair)]

    stages = (
        lambda g: stage_pair(g)[0],
        prepare_a,
        prepare_z,
        prepare_b,
        prepare_z_back,
        prepare_a_back,
        prepare_pair_back,
        lambda g: [],
    )
    flying = [[] for _ in range(GROUPS)]
    level = [0] * GROUPS

    def advance(g):
        if level[g] >= len(stages):
            return
        for c in flying[g]:
            c.wait_recv()
        flying[g] = stages[level[g]](g)
        level[g] += 1
        for c in flying[g]:
            c.start()
        started.extend(flying[g])

    stat_acc[...] = jnp.zeros((TOK, TOK), F32)
    for c in kv_h:
        c.wait_recv()
    for c in qd_h:
        c.start()

    done = set()

    def once(name, action):
        if name not in done:
            done.add(name)
            action()

    def take_kv_w():
        for c in kv_w:
            c.wait_recv()
        for c in kv_c + qd_w:
            c.start()

    def take_kv_c():
        for c in kv_c:
            c.wait_recv()

    for kind, low, high, tiles in segments(sizes, PER):
        if kind >= 1:
            once("kv_w", take_kv_w)
        if kind == 2:
            once("kv_c", take_kv_c)

        @pl.loop(low, high)
        def _(p):
            own_pass(kind, tiles, p)

        if high % PER == 0:
            if high == HEADS:
                stat_ext[4] = jnp.transpose(stat_acc[...])[:32]
                for c in stat_copies:
                    c.start()
            for earlier in range(high // PER):
                advance(earlier)

    for c in qd_w:
        c.wait_recv()
    for c in qd_c:
        c.start()
    for c in qd_h + stat_copies:
        c.wait_recv()
    for kind, low, high, tiles in segments(sizes, 2):
        if kind == 2:
            once("qd_c", lambda: [c.wait_recv() for c in qd_c])
        for g in range(GROUPS):
            advance(g)

        @pl.loop(low, high)
        def _(p):
            owner_pass(kind, tiles, p)

    for _ in stages:
        for g in range(GROUPS):
            advance(g)
    for c in kv_w + kv_h + kv_c + qd_w + qd_h + qd_c + stat_copies + started:
        c.wait_send()
    assert counter[0] <= N_COPIES


N_COPIES = 24 + GROUPS * 25


def finish_kernel(place, attn, gq, gk, gv, text, o_attn, o_gq, o_gk, o_gv, o_tk, o_tv):
    for h in range(HEADS):
        p = place[h]
        for source, out in ((attn, o_attn), (gq, o_gq), (gk, o_gk), (gv, o_gv)):
            out[:, h * HD : (h + 1) * HD] = source[p]
        for side, out in ((0, o_tk), (1, o_tv)):
            out[:, h * HD : (h + 1) * HD] = text[side, p]


VMEM = pl.BlockSpec(memory_space=pltpu.VMEM)
SMEM = pl.BlockSpec(memory_space=pltpu.SMEM)


def fused(number, sizes, operands):
    m_w, m_h = sizes
    n_a = m_w + m_h - HEADS
    halo = [
        pltpu.VMEM((2, 2, m_w, TOK, HD), BF16),
        pltpu.VMEM((2, 2, m_h, TOK, HD), BF16),
        pltpu.VMEM((2, 2, 2, n_a, TOK, HD), BF16),
    ]
    token = jax.ShapeDtypeStruct((HEADS, TOK, HD), BF16)
    return pl.pallas_call(
        functools.partial(main_kernel, sizes),
        out_shape=(token,) * 4 + (jax.ShapeDtypeStruct((2, HEADS, TEXT, HD), BF16),),
        in_specs=[VMEM] * 6,
        out_specs=(VMEM,) * 5,
        scratch_shapes=halo
        + halo
        + [
            pltpu.VMEM((KEYS, HD), BF16),
            pltpu.VMEM((KEYS, HD), BF16),
            pltpu.VMEM((TOK, TOK), F32),
            pltpu.VMEM((9, 32, TOK), F32),
            pltpu.VMEM((HEADS, TEXT, HD), F32),
            pltpu.VMEM((HEADS, TEXT, HD), BF16),
            pltpu.VMEM((HEADS, TEXT, HD), BF16),
            pltpu.VMEM((GROUPS, 3, TEXT, HD), BF16),
            pltpu.VMEM((GROUPS, 3, TEXT, HD), BF16),
            pltpu.VMEM((GROUPS, TEXT, HD), F32),
            pltpu.VMEM((GROUPS, TEXT, HD), BF16),
            pltpu.VMEM((GROUPS, 7, ROWS, HD), BF16),
            pltpu.VMEM((GROUPS, 4, ROWS, HD), BF16),
            pltpu.SemaphoreType.DMA((N_COPIES,)),
            pltpu.SemaphoreType.DMA((N_COPIES,)),
        ],
        compiler_params=pltpu.CompilerParams(
            collective_id=number, has_side_effects=True, vmem_limit_bytes=56 * 1024 * 1024
        ),
    )(*operands)


def finish(place, results):
    token = jax.ShapeDtypeStruct((TOK, CH), BF16)
    rows = jax.ShapeDtypeStruct((TEXT, CH), BF16)
    return pl.pallas_call(
        finish_kernel,
        out_shape=(token, token, token, token, rows, rows),
        in_specs=[SMEM] + [VMEM] * 5,
        out_specs=(VMEM,) * 6,
        compiler_params=pltpu.CompilerParams(vmem_limit_bytes=16 * 1024 * 1024),
    )(place, *results)


def count_of(flags):
    return functools.reduce(jnp.add, flags)


def ready_kernel(
    reach, live, q, k, v, d, tk, tv, mask, kv, qd, text, bias, qbias, pad, place, choice
):
    ha = lax.axis_index("ha")
    wa = lax.axis_index("wa")
    high = [reach[h, 0] for h in range(HEADS)]
    wide = [reach[h, 1] for h in range(HEADS)]
    both = [high[h] * wide[h] for h in range(HEADS)]
    only_h = [high[h] - both[h] for h in range(HEADS)]
    only_w = [wide[h] - both[h] for h in range(HEADS)]
    n_both, n_h, n_w = count_of(both), count_of(only_h), count_of(only_w)

    m_w, m_h, number = jnp.int32(HEADS), jnp.int32(HEADS), jnp.int32(len(VARIANTS) - 1)
    for i in reversed(range(len(VARIANTS) - 1)):
        w, h = VARIANTS[i]
        need = n_both + jnp.maximum(n_w - (HEADS - h), 0) + jnp.maximum(n_h - (HEADS - w), 0)
        fits = need <= w + h - HEADS
        m_w = jnp.where(fits, w, m_w)
        m_h = jnp.where(fits, h, m_h)
        number = jnp.where(fits, i, number)
    choice[0] = number
    room_h, room_w = HEADS - m_w, HEADS - m_h
    in_h, in_w = jnp.minimum(n_h, room_h), jnp.minimum(n_w, room_w)
    first_both = room_h + room_w
    spill_w = first_both + n_both
    spill_h = spill_w + n_w - in_w
    rest = spill_h + n_h - in_h

    seen_both = seen_h = seen_w = seen_none = jnp.int32(0)
    for h in range(HEADS):
        at_h = jnp.where(seen_h < room_h, seen_h, spill_h + seen_h - room_h)
        at_w = jnp.where(seen_w < room_w, room_h + seen_w, spill_w + seen_w - room_w)
        left_h, left_w = room_h - in_h, room_w - in_w
        at_none = jnp.where(
            seen_none < left_h,
            in_h + seen_none,
            jnp.where(
                seen_none < left_h + left_w,
                room_h + in_w + seen_none - left_h,
                rest + seen_none - left_h - left_w,
            ),
        )
        at = jnp.where(
            both[h] == 1,
            first_both + seen_both,
            jnp.where(only_h[h] == 1, at_h, jnp.where(only_w[h] == 1, at_w, at_none)),
        )
        place[h] = at
        seen_both = seen_both + both[h]
        seen_h = seen_h + only_h[h]
        seen_w = seen_w + only_w[h]
        seen_none = seen_none + 1 - both[h] - only_h[h] - only_w[h]

    line = lax.broadcasted_iota(jnp.int32, (TOK, TOK), 0)
    lane = lax.broadcasted_iota(jnp.int32, (TOK, TOK), 1)
    slabs = []
    for dr in (-1, 0, 1):
        row = jnp.clip(ha + dr, 0, 15)
        there = (ha + dr >= 0) & (ha + dr < 16)
        for f in range(2):
            slab = mask[f, pl.ds(pl.multiple_of(row * TH, TH), TH), :]
            slabs.append(jnp.where(there, slab, 0))
    slabs = jnp.concatenate(slabs, axis=0).astype(F32)
    pick = (lax.broadcasted_iota(jnp.int32, (TH, TOK), 1) // TW) % TH
    pick = pick == lax.broadcasted_iota(jnp.int32, (TH, TOK), 0)
    frame = lax.broadcasted_iota(jnp.int32, (1, TOK), 1) // (TH * TW)
    rows = [[None] * 3 for _ in range(3)]
    for j, dc in enumerate((-1, 0, 1)):
        chosen = (line == (wa + dc) * TW + lane % TW).astype(F32)
        spread = jnp.dot(slabs, chosen, preferred_element_type=F32)
        for i in range(3):
            parts = [
                jnp.sum(
                    jnp.where(pick, spread[(i * 2 + f) * TH : (i * 2 + f + 1) * TH], 0.0),
                    axis=0,
                    keepdims=True,
                )
                for f in range(2)
            ]
            rows[i][j] = jnp.where(frame == 0, parts[0], parts[1])
    nine = [rows[i][j] for i in range(3) for j in range(3)]
    column = lax.broadcasted_iota(jnp.int32, (1, TOK), 1)
    words = [(column + i * TOK < live[0]).astype(F32) for i in range(2)]
    table = jnp.concatenate(nine + words + [jnp.zeros((5, TOK), F32)], axis=0)
    pad[...] = jnp.transpose(jnp.broadcast_to(nine[4], (TOK, TOK)))

    tile = lax.broadcasted_iota(jnp.int32, (16, TOK), 0)
    dr, dc = tile // 3 - 1, tile % 3 - 1
    there = (ha + dr >= 0) & (ha + dr < 16) & (wa + dc >= 0) & (wa + dc < 16)
    for h in range(HEADS):
        p = place[h]
        inside = (jnp.abs(dr) <= high[h]) & (jnp.abs(dc) <= wide[h])
        bias[p] = jnp.where((table > 0.5) & (inside | (tile >= 9)), 0.0, -BIG)
        qbias[p] = jnp.where(inside & there, 0.0, BIG)
        for source, out, index in ((k, kv, 0), (v, kv, 1), (q, qd, 0), (d, qd, 1)):
            out[index, p] = source[:, h * HD : (h + 1) * HD]
        for source, index in ((tk, 0), (tv, 1)):
            text[index, p] = source[:, h * HD : (h + 1) * HD]


def ready(reach, live, q, k, v, d, tk, tv, mask):
    tokens = jax.ShapeDtypeStruct((2, HEADS, TOK, HD), BF16)
    rows = jax.ShapeDtypeStruct((HEADS, 16, TOK), F32)
    return pl.pallas_call(
        ready_kernel,
        out_shape=(
            tokens,
            tokens,
            jax.ShapeDtypeStruct((2, HEADS, TEXT, HD), BF16),
            rows,
            rows,
            jax.ShapeDtypeStruct((TOK, TOK), F32),
            jax.ShapeDtypeStruct((HEADS,), jnp.int32),
            jax.ShapeDtypeStruct((1,), jnp.int32),
        ),
        in_specs=[SMEM, SMEM] + [VMEM] * 7,
        out_specs=(VMEM,) * 6 + (SMEM, SMEM),
        compiler_params=pltpu.CompilerParams(vmem_limit_bytes=24 * 1024 * 1024),
    )(reach, live, q, k, v, d, tk, tv, mask)


VARIANTS = ((7, 8), (9, 9), (HEADS, HEADS))


def body(
    query_tokens,
    key_tokens,
    value_tokens,
    grad_output,
    text_keys,
    text_values,
    reach_tiles,
    text_count,
    pad_mask,
):
    shape = query_tokens.shape
    tokens = [t.reshape(TOK, CH) for t in (query_tokens, key_tokens, value_tokens, grad_output)]
    *operands, place, choice = ready(
        reach_tiles, text_count, *tokens, text_keys, text_values, pad_mask
    )

    def variant(number, sizes):
        return lambda place, *operands: finish(place, fused(number, sizes, operands))

    attn, gq, gk, gv, tk, tv = lax.switch(
        choice[0],
        [variant(number, sizes) for number, sizes in enumerate(VARIANTS)],
        place,
        *operands,
    )
    return (
        attn.reshape(shape),
        gq.reshape(shape),
        gk.reshape(shape),
        gv.reshape(shape),
        tk,
        tv,
    )


def solution(mesh):
    tokens = P(None, "ha", "wa", None)
    return jax.shard_map(
        body,
        mesh=mesh,
        in_specs=(tokens,) * 4 + (P(),) * 5,
        out_specs=(tokens,) * 4 + (P(), P()),
        check_vma=False,
    )
```

```python
import functools
import math

import jax
import jax.numpy as jnp
from jax import lax
from jax.experimental import pallas as pl
from jax.experimental.pallas import tpu as pltpu
from jax.sharding import PartitionSpec as P

HEADS = 12
HD = 128
TH = 8
TW = 8
TOK = 128
TEXT = 256
VID = 9 * TOK
KEYS = VID + TEXT
CH = HEADS * HD
GROUPS = 3
PER = HEADS // GROUPS
ROWS = TEXT // 8
IDLE_ROUNDS = 0
SCALE = HD**-0.5
SCALE2 = SCALE * math.log2(math.e)
BIG = 1e30
MESH = pl.DeviceIdType.MESH
F32 = jnp.float32
BF16 = jnp.bfloat16
OFFSETS = tuple((dr, dc) for dr in (-1, 0, 1) for dc in (-1, 0, 1))


def dot_nt(a, b):
    return lax.dot_general(a, b, (((1,), (1,)), ((), ())), preferred_element_type=F32)


def dot_nn(a, b):
    return lax.dot_general(a, b, (((1,), (0,)), ((), ())), preferred_element_type=F32)


def dot_tn(a, b):
    return lax.dot_general(a, b, (((0,), (0,)), ((), ())), preferred_element_type=F32)


def cols(head):
    return pl.ds(pl.multiple_of(head * HD, HD), HD)


class Copy:
    def __init__(self, sems, number, src, dst, device, sends=None, receives=None):
        self.copy = pltpu.make_async_remote_copy(
            src_ref=src,
            dst_ref=dst,
            send_sem=sems[0].at[number],
            recv_sem=sems[1].at[number],
            device_id=device,
            device_id_type=MESH,
        )
        self.sends = sends
        self.receives = receives

    def start(self):
        if self.sends is None:
            self.copy.start()
        else:
            pl.when(self.sends)(self.copy.start)

    def wait_recv(self):
        if self.receives is None:
            self.copy.wait_recv()
        else:
            pl.when(self.receives)(self.copy.wait_recv)

    def wait_send(self):
        if self.sends is None:
            self.copy.wait_send()
        else:
            pl.when(self.sends)(self.copy.wait_send)


def regions(sizes):
    m_w, m_h = sizes
    c, b = HEADS - m_w, HEADS - m_h
    return (
        (range(0, c), (1, 4, 7)),
        (range(c, c + b), (3, 4, 5)),
        (range(c + b, HEADS), tuple(range(9))),
    )


def segments(sizes, step):
    runs = []
    for kind, (span, tiles) in enumerate(regions(sizes)):
        low = span.start
        while low < span.stop:
            high = min(span.stop, (low // step + 1) * step)
            runs.append((kind, low, high, tiles))
            low = high
    return runs


def main_kernel(
    sizes,
    kv_ref,
    qd_ref,
    text_in,
    bias_ref,
    qbias_ref,
    pad_ref,
    attn_ref,
    gq_ref,
    gk_ref,
    gv_ref,
    text_ref,
    kv_rw,
    kv_rh,
    kv_rc,
    qd_rw,
    qd_rh,
    qd_rc,
    left_ext,
    right_ext,
    stat_acc,
    stat_ext,
    own_part,
    pair_src,
    pair_dst,
    a_src,
    a_dst,
    z_acc,
    z_src,
    z_dst,
    b_all,
    send_sems,
    recv_sems,
):
    m_w, m_h = sizes
    n_c, n_b = HEADS - m_w, HEADS - m_h
    n_a = HEADS - n_c - n_b
    ha = lax.axis_index("ha")
    wa = lax.axis_index("wa")
    core = ha % 2
    x = (ha // 2) % 4
    y = (wa // 8) * 2 + ha // 8
    z = wa % 8

    def device(y_, x_, core_, z_):
        return ((y_ % 2) * 8 + x_ * 2 + core_, (y_ // 2) * 8 + z_)

    def a_partner(step):
        along = (core * x + (1 - core) * y + step) % 4
        return along, device(core * y + (1 - core) * along, core * along + (1 - core) * x, core, z)

    def b_partner(step):
        along = (core * y + (1 - core) * x + step) % 4
        return along, device(core * along + (1 - core) * y, core * x + (1 - core) * along, core, z)

    def z_partner(step):
        along = (z + step) % 8
        return along, device(y, x, core, along)

    a_me = core * x + (1 - core) * y
    b_me = core * y + (1 - core) * x
    pair = device(y, x, 1 - core, z)
    has = {-1: (ha > 0, wa > 0), 1: (ha < 15, wa < 15)}

    def exists(dr, dc):
        terms = [has[dr][0]] if dr else []
        terms += [has[dc][1]] if dc else []
        return functools.reduce(jnp.logical_and, terms)

    barrier = pltpu.get_barrier_semaphore()

    def greet(target):
        pl.semaphore_signal(barrier, inc=1, device_id=target, device_id_type=MESH)

    expected = jnp.int32(14)
    for dr, dc in OFFSETS:
        if dr or dc:
            there = exists(dr, dc)
            pl.when(there)(functools.partial(greet, (ha + dr, wa + dc)))
            expected = expected + there.astype(jnp.int32)
    for step in (1, 2, 3):
        greet(a_partner(step)[1])
        greet(b_partner(step)[1])
    for step in range(1, 8):
        greet(z_partner(step)[1])
    greet(pair)

    counter = [0]
    sems = (send_sems, recv_sems)

    def copy(src, dst, target, sends=None, receives=None):
        number = counter[0]
        counter[0] += 1
        return Copy(sems, number, src, dst, target, sends, receives)

    def blank(rw, rh, rc):
        for side, sign in ((0, -1), (1, 1)):

            @pl.when(jnp.logical_not(has[sign][1]))
            def _():
                rw[side] = jnp.zeros(rw.shape[1:], rw.dtype)

            @pl.when(jnp.logical_not(has[sign][0]))
            def _():
                rh[side] = jnp.zeros(rh.shape[1:], rh.dtype)
                rc[side] = jnp.zeros(rc.shape[1:], rc.dtype)

    def halo(own, rw, rh, rc):
        along_w, along_h, corner = [], [], []
        for side, sign in ((0, 1), (1, -1)):
            to, source = has[sign], has[-sign]
            along_w.append(
                copy(own.at[:, pl.ds(n_c, m_w)], rw.at[side], (ha, wa + sign), to[1], source[1])
            )
            for low, count, slot in ((0, n_c, 0), (n_c + n_b, n_a, n_c)):
                if count:
                    along_h.append(
                        copy(
                            own.at[:, pl.ds(low, count)],
                            rh.at[side, :, pl.ds(slot, count)],
                            (ha + sign, wa),
                            to[0],
                            source[0],
                        )
                    )
            corner.append(
                copy(rw.at[:, :, pl.ds(n_b, n_a)], rc.at[side], (ha + sign, wa), to[0], source[0])
            )
        return along_w, along_h, corner

    kv_w, kv_h, kv_c = halo(kv_ref, kv_rw, kv_rh, kv_rc)
    qd_w, qd_h, qd_c = halo(qd_ref, qd_rw, qd_rh, qd_rc)
    stat_copies = [
        copy(
            stat_ext.at[4],
            stat_ext.at[(1 - dr) * 3 + (1 - dc)],
            (ha + dr, wa + dc),
            exists(dr, dc),
            exists(-dr, -dc),
        )
        for dr, dc in OFFSETS
        if dr or dc
    ]

    pl.semaphore_wait(barrier, expected)
    for c in kv_h + kv_w:
        c.start()
    blank(kv_rw, kv_rh, kv_rc)
    blank(qd_rw, qd_rh, qd_rc)
    for dr, dc in OFFSETS:
        if dr or dc:

            @pl.when(jnp.logical_not(exists(dr, dc)))
            def _():
                stat_ext[(dr + 1) * 3 + dc + 1] = jnp.zeros((32, TOK), F32)

    def block(own_ref, index, rw, rh, rc, kind, position, tile):
        dr, dc = OFFSETS[tile]
        if dr == 0 and dc == 0:
            return own_ref[index, position]
        if dr == 0:
            return rw[(dc + 1) // 2, index, position - n_c]
        if dc == 0:
            return rh[(dr + 1) // 2, index, position if kind == 0 else position - n_b]
        return rc[(dr + 1) // 2, (dc + 1) // 2, index, position - n_c - n_b]

    def assemble(ext, first, own_ref, index, rw, rh, rc, kind, position, tiles):
        for i, tile in enumerate(tiles):
            ext[pl.ds(first + i * TOK, TOK), :] = block(
                own_ref, index, rw, rh, rc, kind, position, tile
            )

    lane = lax.broadcasted_iota(jnp.int32, (TOK, TOK), 1)

    def own_pass(kind, tiles, p):
        kv_halo = (kv_rw, kv_rh, kv_rc, kind, p, tiles)
        left_ext[pl.ds(0, TEXT), :] = text_in[0, p]
        right_ext[pl.ds(0, TEXT), :] = text_in[1, p]
        assemble(left_ext, TEXT, kv_ref, 0, *kv_halo)
        assemble(right_ext, TEXT, kv_ref, 1, *kv_halo)
        keys = left_ext[pl.ds(0, TEXT + len(tiles) * TOK), :]
        values = right_ext[pl.ds(0, TEXT + len(tiles) * TOK), :]
        query, grad = qd_ref[0, p], qd_ref[1, p]
        bias = jnp.concatenate([bias_ref[p, pl.ds(t, 1), :] for t in (9, 10) + tiles], axis=1)
        scores = dot_nt(query, keys) * SCALE2 + bias
        highest = jnp.max(scores, axis=1, keepdims=True)
        powers = jnp.exp2(scores - highest)
        total = jnp.sum(powers, axis=1, keepdims=True)
        probs = powers * (1.0 / total)
        probs_b = probs.astype(BF16)
        attn = dot_nn(probs_b, values).astype(BF16)
        attn_ref[p] = attn
        delta = jnp.sum(grad.astype(F32) * attn.astype(F32), axis=1, keepdims=True)
        slopes = (probs * (dot_nt(grad, values) - delta)).astype(BF16)
        gq_ref[p] = (SCALE * dot_nn(slopes, keys)).astype(BF16)
        log_total = highest + jnp.log(total) * math.log2(math.e)
        stat_acc[...] = jnp.where(
            lane == p, log_total, jnp.where(lane == p + 16, delta, stat_acc[...])
        )
        text_k = SCALE * dot_tn(slopes[:, :TEXT], query)
        text_v = dot_tn(probs_b[:, :TEXT], grad)
        own_part[p] = jnp.where(core == 0, text_k, text_v)
        pair_src[p] = jnp.where(core == 0, text_v, text_k).astype(BF16)

    def owner_pass(kind, tiles, p):
        qd_halo = (qd_rw, qd_rh, qd_rc, kind, p, tiles)
        assemble(left_ext, 0, qd_ref, 0, *qd_halo)
        assemble(right_ext, 0, qd_ref, 1, *qd_halo)
        log_total = jnp.concatenate(
            [stat_ext[t, pl.ds(p, 1), :] + qbias_ref[p, pl.ds(t, 1), :] for t in tiles], axis=1
        )
        delta = jnp.concatenate([stat_ext[t, pl.ds(p + 16, 1), :] for t in tiles], axis=1)
        queries = left_ext[pl.ds(0, len(tiles) * TOK), :]
        grads = right_ext[pl.ds(0, len(tiles) * TOK), :]
        probs = jnp.exp2(dot_nt(kv_ref[0, p], queries) * SCALE2 - log_total)
        slopes = (probs * (dot_nt(kv_ref[1, p], grads) - delta)).astype(BF16)
        real = pad_ref[...] > 0
        gk_ref[p] = jnp.where(real, SCALE * dot_nn(slopes, queries), 0.0).astype(BF16)
        gv_ref[p] = jnp.where(real, dot_nn(probs.astype(BF16), grads), 0.0).astype(BF16)

    started = []

    def stage_pair(g):
        span = pl.ds(g * PER, PER)
        made = [copy(pair_src.at[span], pair_dst.at[span], pair)]
        return made, None

    def prepare_a(g):
        for i in range(PER):
            own_part[g * PER + i] = own_part[g * PER + i] + pair_dst[g * PER + i].astype(F32)

        made = []
        for step in (1, 2, 3):
            along, target = a_partner(step)
            a_src[g, step - 1] = own_part[g * PER + along].astype(BF16)
            made.append(copy(a_src.at[g, step - 1], a_dst.at[g, step - 1], target))
        return made

    def prepare_z(g):
        z_acc[g] = (
            own_part[g * PER + a_me]
            + a_dst[g, 0].astype(F32)
            + a_dst[g, 1].astype(F32)
            + a_dst[g, 2].astype(F32)
        )
        z_src[g] = z_acc[g].astype(BF16)
        made = []
        for step in range(1, 8):
            along, target = z_partner(step)
            rows = pl.ds(pl.multiple_of(along * ROWS, ROWS), ROWS)
            made.append(copy(z_src.at[g, rows], z_dst.at[g, step - 1], target))
        return made

    def prepare_b(g):
        total = z_acc[g, pl.ds(pl.multiple_of(z * ROWS, ROWS), ROWS), :]
        for step in range(7):
            total = total + z_dst[g, step].astype(F32)
        b_all[g, b_me] = total.astype(BF16)
        return [
            copy(b_all.at[g, b_me], b_all.at[g, b_me], b_partner(step)[1]) for step in (1, 2, 3)
        ]

    def prepare_z_back(g):
        total = b_all[g, 0].astype(F32)
        for i in (1, 2, 3):
            total = total + b_all[g, i].astype(F32)
        rows = pl.ds(pl.multiple_of(z * ROWS, ROWS), ROWS)
        piece = text_ref.at[core, g * PER + a_me, rows]
        text_ref[core, g * PER + a_me, rows, :] = total.astype(BF16)
        return [copy(piece, piece, z_partner(step)[1]) for step in range(1, 8)]

    def prepare_a_back(g):
        piece = text_ref.at[core, g * PER + a_me]
        return [copy(piece, piece, a_partner(step)[1]) for step in (1, 2, 3)]

    def prepare_pair_back(g):
        piece = text_ref.at[core, pl.ds(g * PER, PER)]
        return [copy(piece, piece, pair)]

    stages = (
        lambda g: stage_pair(g)[0],
        prepare_a,
        prepare_z,
        prepare_b,
        prepare_z_back,
        prepare_a_back,
        prepare_pair_back,
        lambda g: [],
    )
    flying = [[] for _ in range(GROUPS)]
    level = [0] * GROUPS

    def advance(g):
        if level[g] >= len(stages):
            return
        for c in flying[g]:
            c.wait_recv()
        flying[g] = stages[level[g]](g)
        level[g] += 1
        for c in flying[g]:
            c.start()
        started.extend(flying[g])

    stat_acc[...] = jnp.zeros((TOK, TOK), F32)
    for c in kv_h:
        c.wait_recv()

    done = set()

    def once(name, action):
        if name not in done:
            done.add(name)
            action()

    def take_kv_w():
        for c in kv_w:
            c.wait_recv()
        for c in kv_c + qd_w + qd_h:
            c.start()

    def take_kv_c():
        for _ in range(IDLE_ROUNDS):
            for g in range((n_c + n_b) // PER):
                advance(g)
        for c in kv_c:
            c.wait_recv()

    for kind, low, high, tiles in segments(sizes, PER):
        if kind >= 1:
            once("kv_w", take_kv_w)
        if kind == 2:
            once("kv_c", take_kv_c)

        @pl.loop(low, high)
        def _(p):
            own_pass(kind, tiles, p)

        if high % PER == 0:
            if high == HEADS:
                stat_ext[4] = jnp.transpose(stat_acc[...])[:32]
                for c in stat_copies:
                    c.start()
            for earlier in reversed(range(high // PER)):
                advance(earlier)

    for g in reversed(range(GROUPS)):
        advance(g)
    for c in qd_w:
        c.wait_recv()
    for c in qd_c:
        c.start()
    for g in reversed(range(GROUPS)):
        advance(g)
    for c in qd_h + stat_copies:
        c.wait_recv()
    for kind, low, high, tiles in segments(sizes, 2):
        if kind == 2:
            once("qd_c", lambda: [c.wait_recv() for c in qd_c])
        for g in reversed(range(GROUPS)):
            advance(g)

        @pl.loop(low, high)
        def _(p):
            owner_pass(kind, tiles, p)

    for _ in stages:
        for g in range(GROUPS):
            advance(g)
    for c in kv_w + kv_h + kv_c + qd_w + qd_h + qd_c + stat_copies + started:
        c.wait_send()
    assert counter[0] <= N_COPIES


N_COPIES = 24 + GROUPS * 25


def finish_kernel(
    place, attn, gq, gk, gv, text, o_attn, o_gq, o_gk, o_gv, o_tk, o_tv, tokens, words, sems
):
    moves = []
    for i, (source, out) in enumerate(((attn, o_attn), (gq, o_gq), (gk, o_gk), (gv, o_gv))):
        for h in range(HEADS):
            tokens[i, :, h * HD : (h + 1) * HD] = source[place[h]]
        moves.append(pltpu.make_async_copy(tokens.at[i], out, sems.at[i]))
        moves[-1].start()
    for i, out in enumerate((o_tk, o_tv)):
        for h in range(HEADS):
            words[i, :, h * HD : (h + 1) * HD] = text[i, place[h]]
        moves.append(pltpu.make_async_copy(words.at[i], out, sems.at[4 + i]))
        moves[-1].start()
    for move in moves:
        move.wait()


VMEM = pl.BlockSpec(memory_space=pltpu.VMEM)
SMEM = pl.BlockSpec(memory_space=pltpu.SMEM)
HBM = pl.BlockSpec(memory_space=pltpu.HBM)


def fused(number, sizes, operands):
    m_w, m_h = sizes
    n_a = m_w + m_h - HEADS
    halo = [
        pltpu.VMEM((2, 2, m_w, TOK, HD), BF16),
        pltpu.VMEM((2, 2, m_h, TOK, HD), BF16),
        pltpu.VMEM((2, 2, 2, n_a, TOK, HD), BF16),
    ]
    token = jax.ShapeDtypeStruct((HEADS, TOK, HD), BF16)
    return pl.pallas_call(
        functools.partial(main_kernel, sizes),
        out_shape=(token,) * 4 + (jax.ShapeDtypeStruct((2, HEADS, TEXT, HD), BF16),),
        in_specs=[VMEM] * 6,
        out_specs=(VMEM,) * 5,
        scratch_shapes=halo
        + halo
        + [
            pltpu.VMEM((KEYS, HD), BF16),
            pltpu.VMEM((KEYS, HD), BF16),
            pltpu.VMEM((TOK, TOK), F32),
            pltpu.VMEM((9, 32, TOK), F32),
            pltpu.VMEM((HEADS, TEXT, HD), F32),
            pltpu.VMEM((HEADS, TEXT, HD), BF16),
            pltpu.VMEM((HEADS, TEXT, HD), BF16),
            pltpu.VMEM((GROUPS, 3, TEXT, HD), BF16),
            pltpu.VMEM((GROUPS, 3, TEXT, HD), BF16),
            pltpu.VMEM((GROUPS, TEXT, HD), F32),
            pltpu.VMEM((GROUPS, TEXT, HD), BF16),
            pltpu.VMEM((GROUPS, 7, ROWS, HD), BF16),
            pltpu.VMEM((GROUPS, 4, ROWS, HD), BF16),
            pltpu.SemaphoreType.DMA((N_COPIES,)),
            pltpu.SemaphoreType.DMA((N_COPIES,)),
        ],
        compiler_params=pltpu.CompilerParams(
            collective_id=number, has_side_effects=True, vmem_limit_bytes=40 * 1024 * 1024
        ),
    )(*operands)


def finish(place, results):
    token = jax.ShapeDtypeStruct((TOK, CH), BF16)
    rows = jax.ShapeDtypeStruct((TEXT, CH), BF16)
    return pl.pallas_call(
        finish_kernel,
        out_shape=(token, token, token, token, rows, rows),
        in_specs=[SMEM] + [VMEM] * 5,
        out_specs=(HBM,) * 6,
        scratch_shapes=[
            pltpu.VMEM((4, TOK, CH), BF16),
            pltpu.VMEM((2, TEXT, CH), BF16),
            pltpu.SemaphoreType.DMA((6,)),
        ],
        compiler_params=pltpu.CompilerParams(vmem_limit_bytes=16 * 1024 * 1024),
    )(place, *results)


def count_of(flags):
    return functools.reduce(jnp.add, flags)


def ready_kernel(
    reach,
    live,
    q_hbm,
    k_hbm,
    v_hbm,
    d_hbm,
    tk_hbm,
    tv_hbm,
    mask_hbm,
    kv,
    qd,
    text,
    bias,
    qbias,
    pad,
    place,
    choice,
    mask,
    tokens,
    words,
    sems,
):
    k, v, q, d = (tokens.at[i] for i in range(4))
    tk, tv = (words.at[i] for i in range(2))
    moves = [
        pltpu.make_async_copy(source, target, sems.at[i])
        for i, (source, target) in enumerate(
            (
                (mask_hbm, mask),
                (k_hbm, k),
                (v_hbm, v),
                (q_hbm, q),
                (d_hbm, d),
                (tk_hbm, tk),
                (tv_hbm, tv),
            )
        )
    ]
    for move in moves:
        move.start()
    ha = lax.axis_index("ha")
    wa = lax.axis_index("wa")
    high = [reach[h, 0] for h in range(HEADS)]
    wide = [reach[h, 1] for h in range(HEADS)]
    both = [high[h] * wide[h] for h in range(HEADS)]
    only_h = [high[h] - both[h] for h in range(HEADS)]
    only_w = [wide[h] - both[h] for h in range(HEADS)]
    n_both, n_h, n_w = count_of(both), count_of(only_h), count_of(only_w)

    m_w, m_h, number = jnp.int32(HEADS), jnp.int32(HEADS), jnp.int32(len(VARIANTS) - 1)
    for i in reversed(range(len(VARIANTS) - 1)):
        w, h = VARIANTS[i]
        need = n_both + jnp.maximum(n_w - (HEADS - h), 0) + jnp.maximum(n_h - (HEADS - w), 0)
        fits = need <= w + h - HEADS
        m_w = jnp.where(fits, w, m_w)
        m_h = jnp.where(fits, h, m_h)
        number = jnp.where(fits, i, number)
    choice[0] = number
    room_h, room_w = HEADS - m_w, HEADS - m_h
    in_h, in_w = jnp.minimum(n_h, room_h), jnp.minimum(n_w, room_w)
    first_both = room_h + room_w
    spill_w = first_both + n_both
    spill_h = spill_w + n_w - in_w
    rest = spill_h + n_h - in_h

    seen_both = seen_h = seen_w = seen_none = jnp.int32(0)
    for h in range(HEADS):
        at_h = jnp.where(seen_h < room_h, seen_h, spill_h + seen_h - room_h)
        at_w = jnp.where(seen_w < room_w, room_h + seen_w, spill_w + seen_w - room_w)
        left_h, left_w = room_h - in_h, room_w - in_w
        at_none = jnp.where(
            seen_none < left_h,
            in_h + seen_none,
            jnp.where(
                seen_none < left_h + left_w,
                room_h + in_w + seen_none - left_h,
                rest + seen_none - left_h - left_w,
            ),
        )
        at = jnp.where(
            both[h] == 1,
            first_both + seen_both,
            jnp.where(only_h[h] == 1, at_h, jnp.where(only_w[h] == 1, at_w, at_none)),
        )
        place[h] = at
        seen_both = seen_both + both[h]
        seen_h = seen_h + only_h[h]
        seen_w = seen_w + only_w[h]
        seen_none = seen_none + 1 - both[h] - only_h[h] - only_w[h]

    moves[0].wait()
    line = lax.broadcasted_iota(jnp.int32, (TOK, TOK), 0)
    lane = lax.broadcasted_iota(jnp.int32, (TOK, TOK), 1)
    slabs = []
    for dr in (-1, 0, 1):
        row = jnp.clip(ha + dr, 0, 15)
        there = (ha + dr >= 0) & (ha + dr < 16)
        for f in range(2):
            slab = mask[f, pl.ds(pl.multiple_of(row * TH, TH), TH), :]
            slabs.append(jnp.where(there, slab, 0))
    slabs = jnp.concatenate(slabs, axis=0).astype(F32)
    pick = (lax.broadcasted_iota(jnp.int32, (TH, TOK), 1) // TW) % TH
    pick = pick == lax.broadcasted_iota(jnp.int32, (TH, TOK), 0)
    frame = lax.broadcasted_iota(jnp.int32, (1, TOK), 1) // (TH * TW)
    rows = [[None] * 3 for _ in range(3)]
    for j, dc in enumerate((-1, 0, 1)):
        chosen = (line == (wa + dc) * TW + lane % TW).astype(F32)
        spread = jnp.dot(slabs, chosen, preferred_element_type=F32)
        for i in range(3):
            parts = [
                jnp.sum(
                    jnp.where(pick, spread[(i * 2 + f) * TH : (i * 2 + f + 1) * TH], 0.0),
                    axis=0,
                    keepdims=True,
                )
                for f in range(2)
            ]
            rows[i][j] = jnp.where(frame == 0, parts[0], parts[1])
    nine = [rows[i][j] for i in range(3) for j in range(3)]
    column = lax.broadcasted_iota(jnp.int32, (1, TOK), 1)
    words = [(column + i * TOK < live[0]).astype(F32) for i in range(2)]
    table = jnp.concatenate(nine + words + [jnp.zeros((5, TOK), F32)], axis=0)
    pad[...] = jnp.transpose(jnp.broadcast_to(nine[4], (TOK, TOK)))

    tile = lax.broadcasted_iota(jnp.int32, (16, TOK), 0)
    dr, dc = tile // 3 - 1, tile % 3 - 1
    there = (ha + dr >= 0) & (ha + dr < 16) & (wa + dc >= 0) & (wa + dc < 16)
    for h in range(HEADS):
        p = place[h]
        inside = (jnp.abs(dr) <= high[h]) & (jnp.abs(dc) <= wide[h])
        bias[p] = jnp.where((table > 0.5) & (inside | (tile >= 9)), 0.0, -BIG)
        qbias[p] = jnp.where(inside & there, 0.0, BIG)
    for i, (source, out, index) in enumerate(
        ((k, kv, 0), (v, kv, 1), (q, qd, 0), (d, qd, 1), (tk, text, 0), (tv, text, 1))
    ):
        moves[i + 1].wait()
        for h in range(HEADS):
            out[index, place[h]] = source[:, h * HD : (h + 1) * HD]


def ready(reach, live, q, k, v, d, tk, tv, mask):
    tokens = jax.ShapeDtypeStruct((2, HEADS, TOK, HD), BF16)
    rows = jax.ShapeDtypeStruct((HEADS, 16, TOK), F32)
    return pl.pallas_call(
        ready_kernel,
        out_shape=(
            tokens,
            tokens,
            jax.ShapeDtypeStruct((2, HEADS, TEXT, HD), BF16),
            rows,
            rows,
            jax.ShapeDtypeStruct((TOK, TOK), F32),
            jax.ShapeDtypeStruct((HEADS,), jnp.int32),
            jax.ShapeDtypeStruct((1,), jnp.int32),
        ),
        in_specs=[SMEM, SMEM] + [HBM] * 7,
        out_specs=(VMEM,) * 6 + (SMEM, SMEM),
        scratch_shapes=[
            pltpu.VMEM((2, 128, 128), jnp.int32),
            pltpu.VMEM((4, TOK, CH), BF16),
            pltpu.VMEM((2, TEXT, CH), BF16),
            pltpu.SemaphoreType.DMA((7,)),
        ],
        compiler_params=pltpu.CompilerParams(vmem_limit_bytes=24 * 1024 * 1024),
    )(reach, live, *(pltpu.with_memory_space_constraint(x, pltpu.HBM) for x in (q, k, v, d, tk, tv, mask)))


VARIANTS = ((7, 8), (9, 9), (HEADS, HEADS))


def body(
    query_tokens,
    key_tokens,
    value_tokens,
    grad_output,
    text_keys,
    text_values,
    reach_tiles,
    text_count,
    pad_mask,
):
    shape = query_tokens.shape
    tokens = [t.reshape(TOK, CH) for t in (query_tokens, key_tokens, value_tokens, grad_output)]
    *operands, place, choice = ready(
        reach_tiles, text_count, *tokens, text_keys, text_values, pad_mask
    )

    def variant(number, sizes):
        return lambda place, *operands: finish(place, fused(number, sizes, operands))

    attn, gq, gk, gv, tk, tv = lax.switch(
        choice[0],
        [variant(number, sizes) for number, sizes in enumerate(VARIANTS)],
        place,
        *operands,
    )
    return (
        attn.reshape(shape),
        gq.reshape(shape),
        gk.reshape(shape),
        gv.reshape(shape),
        tk,
        tv,
    )


def solution(mesh):
    tokens = P(None, "ha", "wa", None)
    return jax.shard_map(
        body,
        mesh=mesh,
        in_specs=(tokens,) * 4 + (P(),) * 5,
        out_specs=(tokens,) * 4 + (P(), P()),
        check_vma=False,
    )
```

```python
import functools
import math

import jax
import jax.numpy as jnp
from jax import lax
from jax.experimental import pallas as pl
from jax.experimental.pallas import tpu as pltpu
from jax.sharding import PartitionSpec as P

HEADS = 12
HD = 128
TH = 8
TW = 8
TOK = 128
TEXT = 256
VID = 9 * TOK
KEYS = VID + TEXT
CH = HEADS * HD
PLANE = tuple((dy, dx) for dy in range(4) for dx in range(4) if dy or dx)
SCALE = HD**-0.5
SCALE2 = SCALE * math.log2(math.e)
BIG = 1e30
MESH = pl.DeviceIdType.MESH
F32 = jnp.float32
BF16 = jnp.bfloat16
OFFSETS = tuple((dr, dc) for dr in (-1, 0, 1) for dc in (-1, 0, 1))


def dot_nt(a, b):
    return lax.dot_general(a, b, (((1,), (1,)), ((), ())), preferred_element_type=F32)


def dot_nn(a, b):
    return lax.dot_general(a, b, (((1,), (0,)), ((), ())), preferred_element_type=F32)


def dot_tn(a, b):
    return lax.dot_general(a, b, (((0,), (0,)), ((), ())), preferred_element_type=F32)


def cols(head):
    return pl.ds(pl.multiple_of(head * HD, HD), HD)


class Copy:
    def __init__(self, sems, number, src, dst, device, sends=None, receives=None):
        self.copy = pltpu.make_async_remote_copy(
            src_ref=src,
            dst_ref=dst,
            send_sem=sems[0].at[number],
            recv_sem=sems[1].at[number],
            device_id=device,
            device_id_type=MESH,
        )
        self.sends = sends
        self.receives = receives

    def start(self):
        if self.sends is None:
            self.copy.start()
        else:
            pl.when(self.sends)(self.copy.start)

    def wait_recv(self):
        if self.receives is None:
            self.copy.wait_recv()
        else:
            pl.when(self.receives)(self.copy.wait_recv)

    def wait_send(self):
        if self.sends is None:
            self.copy.wait_send()
        else:
            pl.when(self.sends)(self.copy.wait_send)


def regions(sizes):
    m_w, m_h = sizes
    c, b = HEADS - m_w, HEADS - m_h
    return (
        (range(0, c), (1, 4, 7)),
        (range(c, c + b), (3, 4, 5)),
        (range(c + b, HEADS), tuple(range(9))),
    )


def groups(sizes):
    runs = []
    for kind, (span, tiles) in enumerate(regions(sizes)):
        parts = -(-len(span) // 5)
        for i in range(parts):
            low = span.start + i * len(span) // parts
            high = span.start + (i + 1) * len(span) // parts
            runs.append((kind, low, high, tiles))
    return runs


def main_kernel(
    sizes,
    kv_ref,
    qd_ref,
    text_in,
    bias_ref,
    qbias_ref,
    pad_ref,
    attn_ref,
    gq_ref,
    gk_ref,
    gv_ref,
    text_ref,
    kv_rw,
    kv_rh,
    kv_rc,
    qd_rw,
    qd_rh,
    qd_rc,
    left_ext,
    right_ext,
    stat_acc,
    stat_ext,
    own_part,
    pair_src,
    pair_dst,
    a_src,
    a_dst,
    z_all,
    send_sems,
    recv_sems,
):
    m_w, m_h = sizes
    n_c, n_b = HEADS - m_w, HEADS - m_h
    n_a = HEADS - n_c - n_b
    ha = lax.axis_index("ha")
    wa = lax.axis_index("wa")
    core = ha % 2
    x = (ha // 2) % 4
    y = (wa // 8) * 2 + ha // 8
    z = wa % 8

    def device(y_, x_, core_, z_):
        return ((y_ % 2) * 8 + x_ * 2 + core_, (y_ // 2) * 8 + z_)

    def plane_partner(dy, dx):
        y_, x_ = (y + dy) % 4, (x + dx) % 4
        return y_ * 4 + x_, device(y_, x_, core, z)

    def z_partner(step):
        return device(y, x, core, (z + step) % 8)

    me = y * 4 + x
    pair = device(y, x, 1 - core, z)
    has = {-1: (ha > 0, wa > 0), 1: (ha < 15, wa < 15)}

    def exists(dr, dc):
        terms = [has[dr][0]] if dr else []
        terms += [has[dc][1]] if dc else []
        return functools.reduce(jnp.logical_and, terms)

    barrier = pltpu.get_barrier_semaphore()

    def greet(target):
        pl.semaphore_signal(barrier, inc=1, device_id=target, device_id_type=MESH)

    expected = jnp.int32(23)
    for dr, dc in OFFSETS:
        if dr or dc:
            there = exists(dr, dc)
            pl.when(there)(functools.partial(greet, (ha + dr, wa + dc)))
            expected = expected + there.astype(jnp.int32)
    for dy, dx in PLANE:
        greet(plane_partner(dy, dx)[1])
    for step in range(1, 8):
        greet(z_partner(step))
    greet(pair)

    counter = [0]
    sems = (send_sems, recv_sems)

    def copy(src, dst, target, sends=None, receives=None):
        number = counter[0]
        counter[0] += 1
        return Copy(sems, number, src, dst, target, sends, receives)

    def blank(rw, rh, rc):
        for side, sign in ((0, -1), (1, 1)):

            @pl.when(jnp.logical_not(has[sign][1]))
            def _():
                rw[side] = jnp.zeros(rw.shape[1:], rw.dtype)

            @pl.when(jnp.logical_not(has[sign][0]))
            def _():
                rh[side] = jnp.zeros(rh.shape[1:], rh.dtype)
                rc[side] = jnp.zeros(rc.shape[1:], rc.dtype)

    def halo(own, rw, rh, rc):
        along_w, along_h, corner = [], [], []
        for side, sign in ((0, 1), (1, -1)):
            to, source = has[sign], has[-sign]
            along_w.append(
                copy(own.at[:, pl.ds(n_c, m_w)], rw.at[side], (ha, wa + sign), to[1], source[1])
            )
            for low, count, slot in ((0, n_c, 0), (n_c + n_b, n_a, n_c)):
                if count:
                    along_h.append(
                        copy(
                            own.at[:, pl.ds(low, count)],
                            rh.at[side, :, pl.ds(slot, count)],
                            (ha + sign, wa),
                            to[0],
                            source[0],
                        )
                    )
            corner.append(
                copy(rw.at[:, :, pl.ds(n_b, n_a)], rc.at[side], (ha + sign, wa), to[0], source[0])
            )
        return along_w, along_h, corner

    kv_w, kv_h, kv_c = halo(kv_ref, kv_rw, kv_rh, kv_rc)
    qd_w, qd_h, qd_c = halo(qd_ref, qd_rw, qd_rh, qd_rc)
    stat_copies = [
        copy(
            stat_ext.at[4],
            stat_ext.at[(1 - dr) * 3 + (1 - dc)],
            (ha + dr, wa + dc),
            exists(dr, dc),
            exists(-dr, -dc),
        )
        for dr, dc in OFFSETS
        if dr or dc
    ]

    pl.semaphore_wait(barrier, expected)
    for c in kv_h + kv_w:
        c.start()
    blank(kv_rw, kv_rh, kv_rc)
    blank(qd_rw, qd_rh, qd_rc)
    for dr, dc in OFFSETS:
        if dr or dc:

            @pl.when(jnp.logical_not(exists(dr, dc)))
            def _():
                stat_ext[(dr + 1) * 3 + dc + 1] = jnp.zeros((32, TOK), F32)

    def block(own_ref, index, rw, rh, rc, kind, position, tile):
        dr, dc = OFFSETS[tile]
        if dr == 0 and dc == 0:
            return own_ref[index, position]
        if dr == 0:
            return rw[(dc + 1) // 2, index, position - n_c]
        if dc == 0:
            return rh[(dr + 1) // 2, index, position if kind == 0 else position - n_b]
        return rc[(dr + 1) // 2, (dc + 1) // 2, index, position - n_c - n_b]

    def assemble(ext, first, own_ref, index, rw, rh, rc, kind, position, tiles):
        for i, tile in enumerate(tiles):
            ext[pl.ds(first + i * TOK, TOK), :] = block(
                own_ref, index, rw, rh, rc, kind, position, tile
            )

    lane = lax.broadcasted_iota(jnp.int32, (TOK, TOK), 1)

    def own_pass(kind, tiles, p):
        kv_halo = (kv_rw, kv_rh, kv_rc, kind, p, tiles)
        left_ext[pl.ds(0, TEXT), :] = text_in[0, p]
        right_ext[pl.ds(0, TEXT), :] = text_in[1, p]
        assemble(left_ext, TEXT, kv_ref, 0, *kv_halo)
        assemble(right_ext, TEXT, kv_ref, 1, *kv_halo)
        keys = left_ext[pl.ds(0, TEXT + len(tiles) * TOK), :]
        values = right_ext[pl.ds(0, TEXT + len(tiles) * TOK), :]
        query, grad = qd_ref[0, p], qd_ref[1, p]
        bias = jnp.concatenate([bias_ref[p, pl.ds(t, 1), :] for t in (9, 10) + tiles], axis=1)
        scores = dot_nt(query, keys) * SCALE2 + bias
        highest = jnp.max(scores, axis=1, keepdims=True)
        powers = jnp.exp2(scores - highest)
        total = jnp.sum(powers, axis=1, keepdims=True)
        probs = powers * (1.0 / total)
        probs_b = probs.astype(BF16)
        attn = dot_nn(probs_b, values).astype(BF16)
        attn_ref[p] = attn
        delta = jnp.sum(grad.astype(F32) * attn.astype(F32), axis=1, keepdims=True)
        slopes = (probs * (dot_nt(grad, values) - delta)).astype(BF16)
        gq_ref[p] = (SCALE * dot_nn(slopes, keys)).astype(BF16)
        log_total = highest + jnp.log(total) * math.log2(math.e)
        stat_acc[...] = jnp.where(
            lane == p, log_total, jnp.where(lane == p + 16, delta, stat_acc[...])
        )
        text_k = SCALE * dot_tn(slopes[:, :TEXT], query)
        text_v = dot_tn(probs_b[:, :TEXT], grad)
        rows = pl.ds(pl.multiple_of(p * TEXT, TEXT), TEXT)
        own_part[rows, :] = jnp.where(core == 0, text_k, text_v)
        pair_src[rows, :] = jnp.where(core == 0, text_v, text_k).astype(BF16)

    def owner_pass(kind, tiles, p):
        qd_halo = (qd_rw, qd_rh, qd_rc, kind, p, tiles)
        assemble(left_ext, 0, qd_ref, 0, *qd_halo)
        assemble(right_ext, 0, qd_ref, 1, *qd_halo)
        log_total = jnp.concatenate(
            [stat_ext[t, pl.ds(p, 1), :] + qbias_ref[p, pl.ds(t, 1), :] for t in tiles], axis=1
        )
        delta = jnp.concatenate([stat_ext[t, pl.ds(p + 16, 1), :] for t in tiles], axis=1)
        queries = left_ext[pl.ds(0, len(tiles) * TOK), :]
        grads = right_ext[pl.ds(0, len(tiles) * TOK), :]
        probs = jnp.exp2(dot_nt(kv_ref[0, p], queries) * SCALE2 - log_total)
        slopes = (probs * (dot_nt(kv_ref[1, p], grads) - delta)).astype(BF16)
        real = pad_ref[...] > 0
        gk_ref[p] = jnp.where(real, SCALE * dot_nn(slopes, queries), 0.0).astype(BF16)
        gv_ref[p] = jnp.where(real, dot_nn(probs.astype(BF16), grads), 0.0).astype(BF16)

    runs = groups(sizes)
    started = []

    class Bulk:
        def __init__(self, moves, whole):
            number = counter[0]
            counter[0] += 1
            self.copies = [Copy(sems, number, *move) for move in moves]
            self.whole = Copy(sems, number, whole, whole, pair)
            started.append(self)

        def start(self):
            for c in self.copies:
                c.start()

        def wait_recv(self):
            self.whole.wait_recv()

        def wait_send(self):
            self.whole.wait_send()

    def extent(g):
        kind, low, high, tiles = runs[g]
        return low * TEXT, (high - low) * TEXT, (high - low) * (TEXT // 16)

    def part(g, index):
        first, _, rows = extent(g)
        return pl.ds(pl.multiple_of(first + index * rows, 16), rows)

    def within_chip(g):
        first, count, _ = extent(g)
        span = pl.ds(first, count)
        return Bulk([(pair_src.at[span], pair_dst.at[span], pair)], pair_dst.at[span])

    def scatter_plane(g):
        first, count, rows = extent(g)
        for i in range(count // TEXT):
            span = pl.ds(first + i * TEXT, TEXT)
            total = own_part[span, :] + pair_dst[span, :].astype(F32)
            own_part[span, :] = total
            a_src[span, :] = total.astype(BF16)
        moves = []
        for slot, (dy, dx) in enumerate(PLANE):
            index, target = plane_partner(dy, dx)
            moves.append(
                (a_src.at[part(g, index)], a_dst.at[g, slot, pl.ds(0, rows)], target)
            )
        return Bulk(moves, a_dst.at[g, :, pl.ds(0, rows)])

    def along_z(g):
        rows = extent(g)[2]
        total = own_part[part(g, me), :]
        for slot in range(15):
            total = total + a_dst[g, slot, :rows].astype(F32)
        z_all[g, z, :rows] = total.astype(BF16)
        piece = z_all.at[g, z, pl.ds(0, rows)]
        return Bulk(
            [(piece, piece, z_partner(step)) for step in range(1, 8)],
            z_all.at[g, pl.ds(0, 7), pl.ds(0, rows)],
        )

    def gather_plane(g):
        rows = extent(g)[2]
        total = z_all[g, 0, :rows].astype(F32)
        for i in range(1, 8):
            total = total + z_all[g, i, :rows].astype(F32)
        text_ref[core, part(g, me), :] = total.astype(BF16)
        piece = text_ref.at[core, part(g, me)]
        return Bulk(
            [(piece, piece, plane_partner(dy, dx)[1]) for dy, dx in PLANE],
            a_dst.at[g, :, pl.ds(0, rows)],
        )

    def back_within_chip(g):
        first, count, _ = extent(g)
        piece = text_ref.at[core, pl.ds(first, count)]
        return Bulk([(piece, piece, pair)], piece)

    stages = (within_chip, scatter_plane, along_z, gather_plane, back_within_chip)
    flying = [None] * len(runs)
    level = [0] * len(runs)

    def advance(g):
        if level[g] > len(stages):
            return
        if level[g]:
            flying[g].wait_recv()
        if level[g] < len(stages):
            flying[g] = stages[level[g]](g)
            flying[g].start()
        level[g] += 1

    stat_acc[...] = jnp.zeros((TOK, TOK), F32)
    for c in kv_h:
        c.wait_recv()

    done = set()

    def once(name, action):
        if name not in done:
            done.add(name)
            action()

    def take_kv_w():
        for c in kv_w:
            c.wait_recv()
        for c in kv_c + qd_w + qd_h:
            c.start()

    def take_kv_c():
        for c in kv_c:
            c.wait_recv()

    def take_qd_c():
        for c in qd_c:
            c.wait_recv()

    for g, (kind, low, high, tiles) in enumerate(runs):
        if kind >= 1:
            once("kv_w", take_kv_w)
        if kind == 2:
            once("kv_c", take_kv_c)

        @pl.loop(low, high)
        def _(p):
            own_pass(kind, tiles, p)

        if high == HEADS:
            stat_ext[4] = jnp.transpose(stat_acc[...])[:32]
            for c in stat_copies:
                c.start()
        for earlier in reversed(range(g + 1)):
            advance(earlier)

    for g in reversed(range(len(runs))):
        advance(g)
    for c in qd_w:
        c.wait_recv()
    for c in qd_c:
        c.start()
    for c in qd_h + stat_copies:
        c.wait_recv()
    for kind, low, high, tiles in runs:
        if kind == 2:
            once("qd_c", take_qd_c)

        @pl.loop(low, high)
        def _(p):
            owner_pass(kind, tiles, p)

        for g in reversed(range(len(runs))):
            advance(g)

    for _ in range(len(stages)):
        for g in reversed(range(len(runs))):
            advance(g)
    for c in kv_w + kv_h + kv_c + qd_w + qd_h + qd_c + stat_copies + started:
        c.wait_send()
    assert counter[0] <= N_COPIES


N_COPIES = 24 + 20


def finish_kernel(
    place, attn, gq, gk, gv, text, o_attn, o_gq, o_gk, o_gv, o_tk, o_tv, tokens, words, sems
):
    moves = []
    for i, (source, out) in enumerate(((attn, o_attn), (gq, o_gq), (gk, o_gk), (gv, o_gv))):
        for h in range(HEADS):
            tokens[i, :, h * HD : (h + 1) * HD] = source[place[h]]
        moves.append(pltpu.make_async_copy(tokens.at[i], out, sems.at[i]))
        moves[-1].start()
    for i, out in enumerate((o_tk, o_tv)):
        for h in range(HEADS):
            rows = pl.ds(pl.multiple_of(place[h] * TEXT, TEXT), TEXT)
            words[i, :, h * HD : (h + 1) * HD] = text[i, rows, :]
        moves.append(pltpu.make_async_copy(words.at[i], out, sems.at[4 + i]))
        moves[-1].start()
    for move in moves:
        move.wait()


VMEM = pl.BlockSpec(memory_space=pltpu.VMEM)
SMEM = pl.BlockSpec(memory_space=pltpu.SMEM)
HBM = pl.BlockSpec(memory_space=pltpu.HBM)


def fused(number, sizes, operands):
    m_w, m_h = sizes
    n_a = m_w + m_h - HEADS
    runs = groups(sizes)
    rows = max(high - low for _, low, high, _ in runs) * (TEXT // 16)
    halo = [
        pltpu.VMEM((2, 2, m_w, TOK, HD), BF16),
        pltpu.VMEM((2, 2, m_h, TOK, HD), BF16),
        pltpu.VMEM((2, 2, 2, n_a, TOK, HD), BF16),
    ]
    token = jax.ShapeDtypeStruct((HEADS, TOK, HD), BF16)
    return pl.pallas_call(
        functools.partial(main_kernel, sizes),
        out_shape=(token,) * 4 + (jax.ShapeDtypeStruct((2, HEADS * TEXT, HD), BF16),),
        in_specs=[VMEM] * 6,
        out_specs=(VMEM,) * 5,
        scratch_shapes=halo
        + halo
        + [
            pltpu.VMEM((KEYS, HD), BF16),
            pltpu.VMEM((KEYS, HD), BF16),
            pltpu.VMEM((TOK, TOK), F32),
            pltpu.VMEM((9, 32, TOK), F32),
            pltpu.VMEM((HEADS * TEXT, HD), F32),
            pltpu.VMEM((HEADS * TEXT, HD), BF16),
            pltpu.VMEM((HEADS * TEXT, HD), BF16),
            pltpu.VMEM((HEADS * TEXT, HD), BF16),
            pltpu.VMEM((len(runs), 15, rows, HD), BF16),
            pltpu.VMEM((len(runs), 8, rows, HD), BF16),
            pltpu.SemaphoreType.DMA((N_COPIES,)),
            pltpu.SemaphoreType.DMA((N_COPIES,)),
        ],
        compiler_params=pltpu.CompilerParams(
            collective_id=number, has_side_effects=True, vmem_limit_bytes=40 * 1024 * 1024
        ),
    )(*operands)


def finish(place, results):
    token = jax.ShapeDtypeStruct((TOK, CH), BF16)
    rows = jax.ShapeDtypeStruct((TEXT, CH), BF16)
    return pl.pallas_call(
        finish_kernel,
        out_shape=(token, token, token, token, rows, rows),
        in_specs=[SMEM] + [VMEM] * 5,
        out_specs=(HBM,) * 6,
        scratch_shapes=[
            pltpu.VMEM((4, TOK, CH), BF16),
            pltpu.VMEM((2, TEXT, CH), BF16),
            pltpu.SemaphoreType.DMA((6,)),
        ],
        compiler_params=pltpu.CompilerParams(vmem_limit_bytes=16 * 1024 * 1024),
    )(place, *results)


def count_of(flags):
    return functools.reduce(jnp.add, flags)


def ready_kernel(
    reach,
    live,
    q_hbm,
    k_hbm,
    v_hbm,
    d_hbm,
    tk_hbm,
    tv_hbm,
    mask_hbm,
    kv,
    qd,
    text,
    bias,
    qbias,
    pad,
    place,
    choice,
    mask,
    tokens,
    words,
    sems,
):
    k, v, q, d = (tokens.at[i] for i in range(4))
    tk, tv = (words.at[i] for i in range(2))
    moves = [
        pltpu.make_async_copy(source, target, sems.at[i])
        for i, (source, target) in enumerate(
            (
                (mask_hbm, mask),
                (k_hbm, k),
                (v_hbm, v),
                (q_hbm, q),
                (d_hbm, d),
                (tk_hbm, tk),
                (tv_hbm, tv),
            )
        )
    ]
    for move in moves:
        move.start()
    ha = lax.axis_index("ha")
    wa = lax.axis_index("wa")
    high = [reach[h, 0] for h in range(HEADS)]
    wide = [reach[h, 1] for h in range(HEADS)]
    both = [high[h] * wide[h] for h in range(HEADS)]
    only_h = [high[h] - both[h] for h in range(HEADS)]
    only_w = [wide[h] - both[h] for h in range(HEADS)]
    n_both, n_h, n_w = count_of(both), count_of(only_h), count_of(only_w)

    m_w, m_h, number = jnp.int32(HEADS), jnp.int32(HEADS), jnp.int32(len(VARIANTS) - 1)
    for i in reversed(range(len(VARIANTS) - 1)):
        w, h = VARIANTS[i]
        need = n_both + jnp.maximum(n_w - (HEADS - h), 0) + jnp.maximum(n_h - (HEADS - w), 0)
        fits = need <= w + h - HEADS
        m_w = jnp.where(fits, w, m_w)
        m_h = jnp.where(fits, h, m_h)
        number = jnp.where(fits, i, number)
    choice[0] = number
    room_h, room_w = HEADS - m_w, HEADS - m_h
    in_h, in_w = jnp.minimum(n_h, room_h), jnp.minimum(n_w, room_w)
    first_both = room_h + room_w
    spill_w = first_both + n_both
    spill_h = spill_w + n_w - in_w
    rest = spill_h + n_h - in_h

    seen_both = seen_h = seen_w = seen_none = jnp.int32(0)
    for h in range(HEADS):
        at_h = jnp.where(seen_h < room_h, seen_h, spill_h + seen_h - room_h)
        at_w = jnp.where(seen_w < room_w, room_h + seen_w, spill_w + seen_w - room_w)
        left_h, left_w = room_h - in_h, room_w - in_w
        at_none = jnp.where(
            seen_none < left_h,
            in_h + seen_none,
            jnp.where(
                seen_none < left_h + left_w,
                room_h + in_w + seen_none - left_h,
                rest + seen_none - left_h - left_w,
            ),
        )
        at = jnp.where(
            both[h] == 1,
            first_both + seen_both,
            jnp.where(only_h[h] == 1, at_h, jnp.where(only_w[h] == 1, at_w, at_none)),
        )
        place[h] = at
        seen_both = seen_both + both[h]
        seen_h = seen_h + only_h[h]
        seen_w = seen_w + only_w[h]
        seen_none = seen_none + 1 - both[h] - only_h[h] - only_w[h]

    moves[0].wait()
    line = lax.broadcasted_iota(jnp.int32, (TOK, TOK), 0)
    lane = lax.broadcasted_iota(jnp.int32, (TOK, TOK), 1)
    slabs = []
    for dr in (-1, 0, 1):
        row = jnp.clip(ha + dr, 0, 15)
        there = (ha + dr >= 0) & (ha + dr < 16)
        for f in range(2):
            slab = mask[f, pl.ds(pl.multiple_of(row * TH, TH), TH), :]
            slabs.append(jnp.where(there, slab, 0))
    slabs = jnp.concatenate(slabs, axis=0).astype(F32)
    pick = (lax.broadcasted_iota(jnp.int32, (TH, TOK), 1) // TW) % TH
    pick = pick == lax.broadcasted_iota(jnp.int32, (TH, TOK), 0)
    frame = lax.broadcasted_iota(jnp.int32, (1, TOK), 1) // (TH * TW)
    rows = [[None] * 3 for _ in range(3)]
    for j, dc in enumerate((-1, 0, 1)):
        chosen = (line == (wa + dc) * TW + lane % TW).astype(F32)
        spread = jnp.dot(slabs, chosen, preferred_element_type=F32)
        for i in range(3):
            parts = [
                jnp.sum(
                    jnp.where(pick, spread[(i * 2 + f) * TH : (i * 2 + f + 1) * TH], 0.0),
                    axis=0,
                    keepdims=True,
                )
                for f in range(2)
            ]
            rows[i][j] = jnp.where(frame == 0, parts[0], parts[1])
    nine = [rows[i][j] for i in range(3) for j in range(3)]
    column = lax.broadcasted_iota(jnp.int32, (1, TOK), 1)
    words = [(column + i * TOK < live[0]).astype(F32) for i in range(2)]
    table = jnp.concatenate(nine + words + [jnp.zeros((5, TOK), F32)], axis=0)
    pad[...] = jnp.transpose(jnp.broadcast_to(nine[4], (TOK, TOK)))

    tile = lax.broadcasted_iota(jnp.int32, (16, TOK), 0)
    dr, dc = tile // 3 - 1, tile % 3 - 1
    there = (ha + dr >= 0) & (ha + dr < 16) & (wa + dc >= 0) & (wa + dc < 16)
    for h in range(HEADS):
        p = place[h]
        inside = (jnp.abs(dr) <= high[h]) & (jnp.abs(dc) <= wide[h])
        bias[p] = jnp.where((table > 0.5) & (inside | (tile >= 9)), 0.0, -BIG)
        qbias[p] = jnp.where(inside & there, 0.0, BIG)
    for i, (source, out, index) in enumerate(
        ((k, kv, 0), (v, kv, 1), (q, qd, 0), (d, qd, 1), (tk, text, 0), (tv, text, 1))
    ):
        moves[i + 1].wait()
        for h in range(HEADS):
            out[index, place[h]] = source[:, h * HD : (h + 1) * HD]


def ready(reach, live, q, k, v, d, tk, tv, mask):
    tokens = jax.ShapeDtypeStruct((2, HEADS, TOK, HD), BF16)
    rows = jax.ShapeDtypeStruct((HEADS, 16, TOK), F32)
    return pl.pallas_call(
        ready_kernel,
        out_shape=(
            tokens,
            tokens,
            jax.ShapeDtypeStruct((2, HEADS, TEXT, HD), BF16),
            rows,
            rows,
            jax.ShapeDtypeStruct((TOK, TOK), F32),
            jax.ShapeDtypeStruct((HEADS,), jnp.int32),
            jax.ShapeDtypeStruct((1,), jnp.int32),
        ),
        in_specs=[SMEM, SMEM] + [HBM] * 7,
        out_specs=(VMEM,) * 6 + (SMEM, SMEM),
        scratch_shapes=[
            pltpu.VMEM((2, 128, 128), jnp.int32),
            pltpu.VMEM((4, TOK, CH), BF16),
            pltpu.VMEM((2, TEXT, CH), BF16),
            pltpu.SemaphoreType.DMA((7,)),
        ],
        compiler_params=pltpu.CompilerParams(vmem_limit_bytes=24 * 1024 * 1024),
    )(reach, live, *(pltpu.with_memory_space_constraint(x, pltpu.HBM) for x in (q, k, v, d, tk, tv, mask)))


VARIANTS = ((7, 8), (9, 9), (HEADS, HEADS))


def body(
    query_tokens,
    key_tokens,
    value_tokens,
    grad_output,
    text_keys,
    text_values,
    reach_tiles,
    text_count,
    pad_mask,
):
    shape = query_tokens.shape
    tokens = [t.reshape(TOK, CH) for t in (query_tokens, key_tokens, value_tokens, grad_output)]
    *operands, place, choice = ready(
        reach_tiles, text_count, *tokens, text_keys, text_values, pad_mask
    )

    def variant(number, sizes):
        return lambda place, *operands: finish(place, fused(number, sizes, operands))

    attn, gq, gk, gv, tk, tv = lax.switch(
        choice[0],
        [variant(number, sizes) for number, sizes in enumerate(VARIANTS)],
        place,
        *operands,
    )
    return (
        attn.reshape(shape),
        gq.reshape(shape),
        gk.reshape(shape),
        gv.reshape(shape),
        tk,
        tv,
    )


def solution(mesh):
    tokens = P(None, "ha", "wa", None)
    return jax.shard_map(
        body,
        mesh=mesh,
        in_specs=(tokens,) * 4 + (P(),) * 5,
        out_specs=(tokens,) * 4 + (P(), P()),
        check_vma=False,
    )
```

```python
import functools
import math

import jax
import jax.numpy as jnp
from jax import lax
from jax.experimental import pallas as pl
from jax.experimental.pallas import tpu as pltpu
from jax.sharding import PartitionSpec as P

HEADS = 12
HD = 128
TH = 8
TW = 8
TOK = 128
TEXT = 256
VID = 9 * TOK
KEYS = VID + TEXT
CH = HEADS * HD
PLANE = tuple((dy, dx) for dy in range(4) for dx in range(4) if dy or dx)
SCALE = HD**-0.5
SCALE2 = SCALE * math.log2(math.e)
BIG = 1e30
MESH = pl.DeviceIdType.MESH
F32 = jnp.float32
BF16 = jnp.bfloat16
OFFSETS = tuple((dr, dc) for dr in (-1, 0, 1) for dc in (-1, 0, 1))


def dot_nt(a, b):
    return lax.dot_general(a, b, (((1,), (1,)), ((), ())), preferred_element_type=F32)


def dot_nn(a, b):
    return lax.dot_general(a, b, (((1,), (0,)), ((), ())), preferred_element_type=F32)


def dot_tn(a, b):
    return lax.dot_general(a, b, (((0,), (0,)), ((), ())), preferred_element_type=F32)


def cols(head):
    return pl.ds(pl.multiple_of(head * HD, HD), HD)


class Copy:
    def __init__(self, sems, number, src, dst, device, sends=None, receives=None):
        self.copy = pltpu.make_async_remote_copy(
            src_ref=src,
            dst_ref=dst,
            send_sem=sems[0].at[number],
            recv_sem=sems[1].at[number],
            device_id=device,
            device_id_type=MESH,
        )
        self.sends = sends
        self.receives = receives

    def start(self):
        if self.sends is None:
            self.copy.start()
        else:
            pl.when(self.sends)(self.copy.start)

    def wait_recv(self):
        if self.receives is None:
            self.copy.wait_recv()
        else:
            pl.when(self.receives)(self.copy.wait_recv)

    def wait_send(self):
        if self.sends is None:
            self.copy.wait_send()
        else:
            pl.when(self.sends)(self.copy.wait_send)


def regions(sizes):
    m_w, m_h = sizes
    c, b = HEADS - m_w, HEADS - m_h
    return (
        (range(0, c), (1, 4, 7)),
        (range(c, c + b), (3, 4, 5)),
        (range(c + b, HEADS), tuple(range(9))),
    )


def groups(sizes):
    runs = []
    for kind, (span, tiles) in enumerate(regions(sizes)):
        parts = -(-len(span) // 5)
        for i in range(parts):
            low = span.start + i * len(span) // parts
            high = span.start + (i + 1) * len(span) // parts
            runs.append((kind, low, high, tiles))
    return runs


def main_kernel(
    sizes,
    kv_ref,
    qd_ref,
    text_in,
    bias_ref,
    qbias_ref,
    pad_ref,
    attn_ref,
    gq_ref,
    gk_ref,
    gv_ref,
    text_ref,
    kv_rw,
    kv_rh,
    kv_rc,
    qd_rw,
    qd_rh,
    qd_rc,
    left_ext,
    right_ext,
    stat_acc,
    stat_ext,
    own_part,
    pair_src,
    pair_dst,
    a_src,
    a_dst,
    z_all,
    send_sems,
    recv_sems,
):
    m_w, m_h = sizes
    n_c, n_b = HEADS - m_w, HEADS - m_h
    n_a = HEADS - n_c - n_b
    ha = lax.axis_index("ha")
    wa = lax.axis_index("wa")
    core = ha % 2
    x = (ha // 2) % 4
    y = (wa // 8) * 2 + ha // 8
    z = wa % 8

    def device(y_, x_, core_, z_):
        return ((y_ % 2) * 8 + x_ * 2 + core_, (y_ // 2) * 8 + z_)

    def plane_partner(dy, dx):
        y_, x_ = (y + dy) % 4, (x + dx) % 4
        return x_ * 4 + y_, device(y_, x_, core, z)

    def z_partner(step):
        return device(y, x, core, (z + step) % 8)

    me = x * 4 + y
    pair = device(y, x, 1 - core, z)
    has = {-1: (ha > 0, wa > 0), 1: (ha < 15, wa < 15)}

    def exists(dr, dc):
        terms = [has[dr][0]] if dr else []
        terms += [has[dc][1]] if dc else []
        return functools.reduce(jnp.logical_and, terms)

    barrier = pltpu.get_barrier_semaphore()

    def greet(target):
        pl.semaphore_signal(barrier, inc=1, device_id=target, device_id_type=MESH)

    expected = jnp.int32(23)
    for dr, dc in OFFSETS:
        if dr or dc:
            there = exists(dr, dc)
            pl.when(there)(functools.partial(greet, (ha + dr, wa + dc)))
            expected = expected + there.astype(jnp.int32)
    for dy, dx in PLANE:
        greet(plane_partner(dy, dx)[1])
    for step in range(1, 8):
        greet(z_partner(step))
    greet(pair)

    counter = [0]
    sems = (send_sems, recv_sems)

    def copy(src, dst, target, sends=None, receives=None):
        number = counter[0]
        counter[0] += 1
        return Copy(sems, number, src, dst, target, sends, receives)

    def blank(rw, rh, rc):
        for side, sign in ((0, -1), (1, 1)):

            @pl.when(jnp.logical_not(has[sign][1]))
            def _():
                rw[side] = jnp.zeros(rw.shape[1:], rw.dtype)

            @pl.when(jnp.logical_not(has[sign][0]))
            def _():
                rh[side] = jnp.zeros(rh.shape[1:], rh.dtype)
                rc[side] = jnp.zeros(rc.shape[1:], rc.dtype)

    def halo(own, rw, rh, rc):
        along_w, along_h, corner = [], [], []
        for side, sign in ((0, 1), (1, -1)):
            to, source = has[sign], has[-sign]
            along_w.append(
                copy(own.at[:, pl.ds(n_c, m_w)], rw.at[side], (ha, wa + sign), to[1], source[1])
            )
            for low, count, slot in ((0, n_c, 0), (n_c + n_b, n_a, n_c)):
                if count:
                    along_h.append(
                        copy(
                            own.at[:, pl.ds(low, count)],
                            rh.at[side, :, pl.ds(slot, count)],
                            (ha + sign, wa),
                            to[0],
                            source[0],
                        )
                    )
            corner.append(
                copy(rw.at[:, :, pl.ds(n_b, n_a)], rc.at[side], (ha + sign, wa), to[0], source[0])
            )
        return along_w, along_h, corner

    kv_w, kv_h, kv_c = halo(kv_ref, kv_rw, kv_rh, kv_rc)
    qd_w, qd_h, qd_c = halo(qd_ref, qd_rw, qd_rh, qd_rc)
    stat_copies = [
        copy(
            stat_ext.at[4],
            stat_ext.at[(1 - dr) * 3 + (1 - dc)],
            (ha + dr, wa + dc),
            exists(dr, dc),
            exists(-dr, -dc),
        )
        for dr, dc in OFFSETS
        if dr or dc
    ]

    pl.semaphore_wait(barrier, expected)
    for c in kv_h + kv_w:
        c.start()
    blank(kv_rw, kv_rh, kv_rc)
    blank(qd_rw, qd_rh, qd_rc)
    for dr, dc in OFFSETS:
        if dr or dc:

            @pl.when(jnp.logical_not(exists(dr, dc)))
            def _():
                stat_ext[(dr + 1) * 3 + dc + 1] = jnp.zeros((32, TOK), F32)

    def block(own_ref, index, rw, rh, rc, kind, position, tile):
        dr, dc = OFFSETS[tile]
        if dr == 0 and dc == 0:
            return own_ref[index, position]
        if dr == 0:
            return rw[(dc + 1) // 2, index, position - n_c]
        if dc == 0:
            return rh[(dr + 1) // 2, index, position if kind == 0 else position - n_b]
        return rc[(dr + 1) // 2, (dc + 1) // 2, index, position - n_c - n_b]

    def assemble(ext, first, own_ref, index, rw, rh, rc, kind, position, tiles):
        for i, tile in enumerate(tiles):
            ext[pl.ds(first + i * TOK, TOK), :] = block(
                own_ref, index, rw, rh, rc, kind, position, tile
            )

    lane = lax.broadcasted_iota(jnp.int32, (TOK, TOK), 1)

    def own_pass(kind, tiles, p):
        kv_halo = (kv_rw, kv_rh, kv_rc, kind, p, tiles)
        left_ext[pl.ds(0, TEXT), :] = text_in[0, p]
        right_ext[pl.ds(0, TEXT), :] = text_in[1, p]
        assemble(left_ext, TEXT, kv_ref, 0, *kv_halo)
        assemble(right_ext, TEXT, kv_ref, 1, *kv_halo)
        keys = left_ext[pl.ds(0, TEXT + len(tiles) * TOK), :]
        values = right_ext[pl.ds(0, TEXT + len(tiles) * TOK), :]
        query, grad = qd_ref[0, p], qd_ref[1, p]
        bias = jnp.concatenate([bias_ref[p, pl.ds(t, 1), :] for t in (9, 10) + tiles], axis=1)
        scores = dot_nt(query, keys) * SCALE2 + bias
        highest = jnp.max(scores, axis=1, keepdims=True)
        powers = jnp.exp2(scores - highest)
        total = jnp.sum(powers, axis=1, keepdims=True)
        probs = powers * (1.0 / total)
        probs_b = probs.astype(BF16)
        attn = dot_nn(probs_b, values).astype(BF16)
        attn_ref[p] = attn
        delta = jnp.sum(grad.astype(F32) * attn.astype(F32), axis=1, keepdims=True)
        slopes = (probs * (dot_nt(grad, values) - delta)).astype(BF16)
        gq_ref[p] = (SCALE * dot_nn(slopes, keys)).astype(BF16)
        log_total = highest + jnp.log(total) * math.log2(math.e)
        stat_acc[...] = jnp.where(
            lane == p, log_total, jnp.where(lane == p + 16, delta, stat_acc[...])
        )
        text_k = SCALE * dot_tn(slopes[:, :TEXT], query)
        text_v = dot_tn(probs_b[:, :TEXT], grad)
        rows = pl.ds(pl.multiple_of(p * TEXT, TEXT), TEXT)
        own_part[rows, :] = jnp.where(core == 0, text_k, text_v)
        pair_src[rows, :] = jnp.where(core == 0, text_v, text_k).astype(BF16)

    def owner_pass(kind, tiles, p):
        qd_halo = (qd_rw, qd_rh, qd_rc, kind, p, tiles)
        assemble(left_ext, 0, qd_ref, 0, *qd_halo)
        assemble(right_ext, 0, qd_ref, 1, *qd_halo)
        log_total = jnp.concatenate(
            [stat_ext[t, pl.ds(p, 1), :] + qbias_ref[p, pl.ds(t, 1), :] for t in tiles], axis=1
        )
        delta = jnp.concatenate([stat_ext[t, pl.ds(p + 16, 1), :] for t in tiles], axis=1)
        queries = left_ext[pl.ds(0, len(tiles) * TOK), :]
        grads = right_ext[pl.ds(0, len(tiles) * TOK), :]
        probs = jnp.exp2(dot_nt(kv_ref[0, p], queries) * SCALE2 - log_total)
        slopes = (probs * (dot_nt(kv_ref[1, p], grads) - delta)).astype(BF16)
        real = pad_ref[...] > 0
        gk_ref[p] = jnp.where(real, SCALE * dot_nn(slopes, queries), 0.0).astype(BF16)
        gv_ref[p] = jnp.where(real, dot_nn(probs.astype(BF16), grads), 0.0).astype(BF16)

    runs = groups(sizes)
    started = []

    class Bulk:
        def __init__(self, moves, whole):
            number = counter[0]
            counter[0] += 1
            self.copies = [Copy(sems, number, *move) for move in moves]
            self.whole = Copy(sems, number, whole, whole, pair)
            started.append(self)

        def start(self):
            for c in self.copies:
                c.start()

        def wait_recv(self):
            self.whole.wait_recv()

        def wait_send(self):
            self.whole.wait_send()

    def extent(g):
        kind, low, high, tiles = runs[g]
        return low * TEXT, (high - low) * TEXT, (high - low) * (TEXT // 16)

    def part(g, index):
        first, _, rows = extent(g)
        return pl.ds(pl.multiple_of(first + index * rows, 16), rows)

    def within_chip(g):
        first, count, _ = extent(g)
        span = pl.ds(first, count)
        return Bulk([(pair_src.at[span], pair_dst.at[span], pair)], pair_dst.at[span])

    def add_pair(g):
        first, count, _ = extent(g)
        for i in range(count // TEXT):
            span = pl.ds(first + i * TEXT, TEXT)
            total = own_part[span, :] + pair_dst[span, :].astype(F32)
            own_part[span, :] = total
            a_src[span, :] = total.astype(BF16)

    def quarter(g, index):
        first, _, rows = extent(g)
        return pl.ds(pl.multiple_of(first + index * 4 * rows, 16), 4 * rows)

    def landing(g, low, high):
        rows = extent(g)[2]
        return a_dst.at[g, pl.ds(low * rows, (high - low) * rows)]

    def scatter_plane(g):
        add_pair(g)
        moves = []
        for slot, (dy, dx) in enumerate(PLANE):
            index, target = plane_partner(dy, dx)
            moves.append((a_src.at[part(g, index)], landing(g, slot, slot + 1), target))
        return Bulk(moves, landing(g, 0, 15))

    def scatter_x(g):
        add_pair(g)
        moves = []
        for slot, step in enumerate((1, 2, 3)):
            target = plane_partner(0, step)[1]
            moves.append(
                (
                    a_src.at[quarter(g, (x + step) % 4)],
                    landing(g, 4 * slot, 4 * slot + 4),
                    target,
                )
            )
        return Bulk(moves, landing(g, 0, 12))

    def scatter_y(g):
        rows = extent(g)[2]
        total = own_part[quarter(g, x), :]
        for slot in range(3):
            total = total + a_dst[g, 4 * slot * rows : (4 * slot + 4) * rows, :].astype(F32)
        own_part[quarter(g, x), :] = total
        a_src[quarter(g, x), :] = total.astype(BF16)
        moves = []
        for slot, step in enumerate((1, 2, 3)):
            index, target = plane_partner(step, 0)
            moves.append((a_src.at[part(g, index)], landing(g, 12 + slot, 13 + slot), target))
        return Bulk(moves, landing(g, 12, 15))

    def along_z(g):
        rows = extent(g)[2]
        total = own_part[part(g, me), :]
        for slot in range(0 if is_last(g) else 12, 15):
            total = total + a_dst[g, slot * rows : (slot + 1) * rows, :].astype(F32)
        z_all[g, z, :rows] = total.astype(BF16)
        piece = z_all.at[g, z, pl.ds(0, rows)]
        return Bulk(
            [(piece, piece, z_partner(step)) for step in range(1, 8)],
            z_all.at[g, pl.ds(0, 7), pl.ds(0, rows)],
        )

    def sum_z(g):
        rows = extent(g)[2]
        total = z_all[g, 0, :rows].astype(F32)
        for i in range(1, 8):
            total = total + z_all[g, i, :rows].astype(F32)
        text_ref[core, part(g, me), :] = total.astype(BF16)
        return text_ref.at[core, part(g, me)]

    def gather_plane(g):
        piece = sum_z(g)
        return Bulk(
            [(piece, piece, plane_partner(dy, dx)[1]) for dy, dx in PLANE], landing(g, 0, 15)
        )

    def gather_y(g):
        piece = sum_z(g)
        return Bulk(
            [(piece, piece, plane_partner(step, 0)[1]) for step in (1, 2, 3)], landing(g, 0, 3)
        )

    def gather_x(g):
        piece = text_ref.at[core, quarter(g, x)]
        return Bulk(
            [(piece, piece, plane_partner(0, step)[1]) for step in (1, 2, 3)], landing(g, 0, 12)
        )

    def back_within_chip(g):
        first, count, _ = extent(g)
        piece = text_ref.at[core, pl.ds(first, count)]
        return Bulk([(piece, piece, pair)], piece)

    quick = (within_chip, scatter_plane, along_z, gather_plane, back_within_chip)
    light = (
        within_chip,
        scatter_x,
        scatter_y,
        along_z,
        gather_y,
        gather_x,
        back_within_chip,
    )

    def is_last(g):
        return g == len(runs) - 1

    flying = [None] * len(runs)
    level = [0] * len(runs)

    def advance(g):
        stages = quick if is_last(g) else light
        if level[g] > len(stages):
            return
        if level[g]:
            flying[g].wait_recv()
        if level[g] < len(stages):
            flying[g] = stages[level[g]](g)
            flying[g].start()
        level[g] += 1

    stat_acc[...] = jnp.zeros((TOK, TOK), F32)
    for c in kv_h:
        c.wait_recv()

    done = set()

    def once(name, action):
        if name not in done:
            done.add(name)
            action()

    def take_kv_w():
        for c in kv_w:
            c.wait_recv()
        for c in kv_c + qd_w:
            c.start()

    def take_kv_c():
        for c in kv_c:
            c.wait_recv()
        for c in qd_h:
            c.start()

    def take_qd_c():
        for c in qd_c:
            c.wait_recv()

    for g, (kind, low, high, tiles) in enumerate(runs):
        if kind >= 1:
            once("kv_w", take_kv_w)
        if kind == 2:
            once("kv_c", take_kv_c)

        @pl.loop(low, high)
        def _(p):
            own_pass(kind, tiles, p)

        if high == HEADS:
            stat_ext[4] = jnp.transpose(stat_acc[...])[:32]
            for c in stat_copies:
                c.start()
        for earlier in reversed(range(g + 1)):
            advance(earlier)

    for g in reversed(range(len(runs))):
        advance(g)
    for c in qd_w:
        c.wait_recv()
    for c in qd_c:
        c.start()
    for c in qd_h + stat_copies:
        c.wait_recv()
    for kind, low, high, tiles in runs:
        if kind == 2:
            once("qd_c", take_qd_c)

        @pl.loop(low, high)
        def _(p):
            owner_pass(kind, tiles, p)

        for g in reversed(range(len(runs))):
            advance(g)

    for _ in range(len(light)):
        for g in reversed(range(len(runs))):
            advance(g)
    for c in kv_w + kv_h + kv_c + qd_w + qd_h + qd_c + stat_copies + started:
        c.wait_send()
    assert counter[0] <= N_COPIES


N_COPIES = 24 + 28


def finish_kernel(
    place, attn, gq, gk, gv, text, o_attn, o_gq, o_gk, o_gv, o_tk, o_tv, tokens, words, sems
):
    moves = []
    for i, (source, out) in enumerate(((attn, o_attn), (gq, o_gq), (gk, o_gk), (gv, o_gv))):
        for h in range(HEADS):
            tokens[i, :, h * HD : (h + 1) * HD] = source[place[h]]
        moves.append(pltpu.make_async_copy(tokens.at[i], out, sems.at[i]))
        moves[-1].start()
    for i, out in enumerate((o_tk, o_tv)):
        for h in range(HEADS):
            rows = pl.ds(pl.multiple_of(place[h] * TEXT, TEXT), TEXT)
            words[i, :, h * HD : (h + 1) * HD] = text[i, rows, :]
        moves.append(pltpu.make_async_copy(words.at[i], out, sems.at[4 + i]))
        moves[-1].start()
    for move in moves:
        move.wait()


VMEM = pl.BlockSpec(memory_space=pltpu.VMEM)
SMEM = pl.BlockSpec(memory_space=pltpu.SMEM)
HBM = pl.BlockSpec(memory_space=pltpu.HBM)


def fused(number, sizes, operands):
    m_w, m_h = sizes
    n_a = m_w + m_h - HEADS
    runs = groups(sizes)
    rows = max(high - low for _, low, high, _ in runs) * (TEXT // 16)
    halo = [
        pltpu.VMEM((2, 2, m_w, TOK, HD), BF16),
        pltpu.VMEM((2, 2, m_h, TOK, HD), BF16),
        pltpu.VMEM((2, 2, 2, n_a, TOK, HD), BF16),
    ]
    token = jax.ShapeDtypeStruct((HEADS, TOK, HD), BF16)
    return pl.pallas_call(
        functools.partial(main_kernel, sizes),
        out_shape=(token,) * 4 + (jax.ShapeDtypeStruct((2, HEADS * TEXT, HD), BF16),),
        in_specs=[VMEM] * 6,
        out_specs=(VMEM,) * 5,
        scratch_shapes=halo
        + halo
        + [
            pltpu.VMEM((KEYS, HD), BF16),
            pltpu.VMEM((KEYS, HD), BF16),
            pltpu.VMEM((TOK, TOK), F32),
            pltpu.VMEM((9, 32, TOK), F32),
            pltpu.VMEM((HEADS * TEXT, HD), F32),
            pltpu.VMEM((HEADS * TEXT, HD), BF16),
            pltpu.VMEM((HEADS * TEXT, HD), BF16),
            pltpu.VMEM((HEADS * TEXT, HD), BF16),
            pltpu.VMEM((len(runs), 15 * rows, HD), BF16),
            pltpu.VMEM((len(runs), 8, rows, HD), BF16),
            pltpu.SemaphoreType.DMA((N_COPIES,)),
            pltpu.SemaphoreType.DMA((N_COPIES,)),
        ],
        compiler_params=pltpu.CompilerParams(
            collective_id=number, has_side_effects=True, vmem_limit_bytes=40 * 1024 * 1024
        ),
    )(*operands)


def finish(place, results):
    token = jax.ShapeDtypeStruct((TOK, CH), BF16)
    rows = jax.ShapeDtypeStruct((TEXT, CH), BF16)
    return pl.pallas_call(
        finish_kernel,
        out_shape=(token, token, token, token, rows, rows),
        in_specs=[SMEM] + [VMEM] * 5,
        out_specs=(HBM,) * 6,
        scratch_shapes=[
            pltpu.VMEM((4, TOK, CH), BF16),
            pltpu.VMEM((2, TEXT, CH), BF16),
            pltpu.SemaphoreType.DMA((6,)),
        ],
        compiler_params=pltpu.CompilerParams(vmem_limit_bytes=16 * 1024 * 1024),
    )(place, *results)


def count_of(flags):
    return functools.reduce(jnp.add, flags)


def ready_kernel(
    reach,
    live,
    q_hbm,
    k_hbm,
    v_hbm,
    d_hbm,
    tk_hbm,
    tv_hbm,
    mask_hbm,
    kv,
    qd,
    text,
    bias,
    qbias,
    pad,
    place,
    choice,
    mask,
    tokens,
    words,
    sems,
):
    k, v, q, d = (tokens.at[i] for i in range(4))
    tk, tv = (words.at[i] for i in range(2))
    moves = [
        pltpu.make_async_copy(source, target, sems.at[i])
        for i, (source, target) in enumerate(
            (
                (mask_hbm, mask),
                (k_hbm, k),
                (v_hbm, v),
                (q_hbm, q),
                (d_hbm, d),
                (tk_hbm, tk),
                (tv_hbm, tv),
            )
        )
    ]
    for move in moves:
        move.start()
    ha = lax.axis_index("ha")
    wa = lax.axis_index("wa")
    high = [reach[h, 0] for h in range(HEADS)]
    wide = [reach[h, 1] for h in range(HEADS)]
    both = [high[h] * wide[h] for h in range(HEADS)]
    only_h = [high[h] - both[h] for h in range(HEADS)]
    only_w = [wide[h] - both[h] for h in range(HEADS)]
    n_both, n_h, n_w = count_of(both), count_of(only_h), count_of(only_w)

    m_w, m_h, number = jnp.int32(HEADS), jnp.int32(HEADS), jnp.int32(len(VARIANTS) - 1)
    for i in reversed(range(len(VARIANTS) - 1)):
        w, h = VARIANTS[i]
        need = n_both + jnp.maximum(n_w - (HEADS - h), 0) + jnp.maximum(n_h - (HEADS - w), 0)
        fits = need <= w + h - HEADS
        m_w = jnp.where(fits, w, m_w)
        m_h = jnp.where(fits, h, m_h)
        number = jnp.where(fits, i, number)
    choice[0] = number
    room_h, room_w = HEADS - m_w, HEADS - m_h
    in_h, in_w = jnp.minimum(n_h, room_h), jnp.minimum(n_w, room_w)
    first_both = room_h + room_w
    spill_w = first_both + n_both
    spill_h = spill_w + n_w - in_w
    rest = spill_h + n_h - in_h

    seen_both = seen_h = seen_w = seen_none = jnp.int32(0)
    for h in range(HEADS):
        at_h = jnp.where(seen_h < room_h, seen_h, spill_h + seen_h - room_h)
        at_w = jnp.where(seen_w < room_w, room_h + seen_w, spill_w + seen_w - room_w)
        left_h, left_w = room_h - in_h, room_w - in_w
        at_none = jnp.where(
            seen_none < left_h,
            in_h + seen_none,
            jnp.where(
                seen_none < left_h + left_w,
                room_h + in_w + seen_none - left_h,
                rest + seen_none - left_h - left_w,
            ),
        )
        at = jnp.where(
            both[h] == 1,
            first_both + seen_both,
            jnp.where(only_h[h] == 1, at_h, jnp.where(only_w[h] == 1, at_w, at_none)),
        )
        place[h] = at
        seen_both = seen_both + both[h]
        seen_h = seen_h + only_h[h]
        seen_w = seen_w + only_w[h]
        seen_none = seen_none + 1 - both[h] - only_h[h] - only_w[h]

    moves[0].wait()
    line = lax.broadcasted_iota(jnp.int32, (TOK, TOK), 0)
    lane = lax.broadcasted_iota(jnp.int32, (TOK, TOK), 1)
    slabs = []
    for dr in (-1, 0, 1):
        row = jnp.clip(ha + dr, 0, 15)
        there = (ha + dr >= 0) & (ha + dr < 16)
        for f in range(2):
            slab = mask[f, pl.ds(pl.multiple_of(row * TH, TH), TH), :]
            slabs.append(jnp.where(there, slab, 0))
    slabs = jnp.concatenate(slabs, axis=0).astype(F32)
    pick = (lax.broadcasted_iota(jnp.int32, (TH, TOK), 1) // TW) % TH
    pick = pick == lax.broadcasted_iota(jnp.int32, (TH, TOK), 0)
    frame = lax.broadcasted_iota(jnp.int32, (1, TOK), 1) // (TH * TW)
    rows = [[None] * 3 for _ in range(3)]
    for j, dc in enumerate((-1, 0, 1)):
        chosen = (line == (wa + dc) * TW + lane % TW).astype(F32)
        spread = jnp.dot(slabs, chosen, preferred_element_type=F32)
        for i in range(3):
            parts = [
                jnp.sum(
                    jnp.where(pick, spread[(i * 2 + f) * TH : (i * 2 + f + 1) * TH], 0.0),
                    axis=0,
                    keepdims=True,
                )
                for f in range(2)
            ]
            rows[i][j] = jnp.where(frame == 0, parts[0], parts[1])
    nine = [rows[i][j] for i in range(3) for j in range(3)]
    column = lax.broadcasted_iota(jnp.int32, (1, TOK), 1)
    words = [(column + i * TOK < live[0]).astype(F32) for i in range(2)]
    table = jnp.concatenate(nine + words + [jnp.zeros((5, TOK), F32)], axis=0)
    pad[...] = jnp.transpose(jnp.broadcast_to(nine[4], (TOK, TOK)))

    tile = lax.broadcasted_iota(jnp.int32, (16, TOK), 0)
    dr, dc = tile // 3 - 1, tile % 3 - 1
    there = (ha + dr >= 0) & (ha + dr < 16) & (wa + dc >= 0) & (wa + dc < 16)
    for h in range(HEADS):
        p = place[h]
        inside = (jnp.abs(dr) <= high[h]) & (jnp.abs(dc) <= wide[h])
        bias[p] = jnp.where((table > 0.5) & (inside | (tile >= 9)), 0.0, -BIG)
        qbias[p] = jnp.where(inside & there, 0.0, BIG)
    for i, (source, out, index) in enumerate(
        ((k, kv, 0), (v, kv, 1), (q, qd, 0), (d, qd, 1), (tk, text, 0), (tv, text, 1))
    ):
        moves[i + 1].wait()
        for h in range(HEADS):
            out[index, place[h]] = source[:, h * HD : (h + 1) * HD]


def ready(reach, live, q, k, v, d, tk, tv, mask):
    tokens = jax.ShapeDtypeStruct((2, HEADS, TOK, HD), BF16)
    rows = jax.ShapeDtypeStruct((HEADS, 16, TOK), F32)
    return pl.pallas_call(
        ready_kernel,
        out_shape=(
            tokens,
            tokens,
            jax.ShapeDtypeStruct((2, HEADS, TEXT, HD), BF16),
            rows,
            rows,
            jax.ShapeDtypeStruct((TOK, TOK), F32),
            jax.ShapeDtypeStruct((HEADS,), jnp.int32),
            jax.ShapeDtypeStruct((1,), jnp.int32),
        ),
        in_specs=[SMEM, SMEM] + [HBM] * 7,
        out_specs=(VMEM,) * 6 + (SMEM, SMEM),
        scratch_shapes=[
            pltpu.VMEM((2, 128, 128), jnp.int32),
            pltpu.VMEM((4, TOK, CH), BF16),
            pltpu.VMEM((2, TEXT, CH), BF16),
            pltpu.SemaphoreType.DMA((7,)),
        ],
        compiler_params=pltpu.CompilerParams(vmem_limit_bytes=24 * 1024 * 1024),
    )(reach, live, *(pltpu.with_memory_space_constraint(x, pltpu.HBM) for x in (q, k, v, d, tk, tv, mask)))


VARIANTS = ((7, 8), (9, 9), (HEADS, HEADS))


def body(
    query_tokens,
    key_tokens,
    value_tokens,
    grad_output,
    text_keys,
    text_values,
    reach_tiles,
    text_count,
    pad_mask,
):
    shape = query_tokens.shape
    tokens = [t.reshape(TOK, CH) for t in (query_tokens, key_tokens, value_tokens, grad_output)]
    *operands, place, choice = ready(
        reach_tiles, text_count, *tokens, text_keys, text_values, pad_mask
    )

    def variant(number, sizes):
        return lambda place, *operands: finish(place, fused(number, sizes, operands))

    attn, gq, gk, gv, tk, tv = lax.switch(
        choice[0],
        [variant(number, sizes) for number, sizes in enumerate(VARIANTS)],
        place,
        *operands,
    )
    return (
        attn.reshape(shape),
        gq.reshape(shape),
        gk.reshape(shape),
        gv.reshape(shape),
        tk,
        tv,
    )


def solution(mesh):
    tokens = P(None, "ha", "wa", None)
    return jax.shard_map(
        body,
        mesh=mesh,
        in_specs=(tokens,) * 4 + (P(),) * 5,
        out_specs=(tokens,) * 4 + (P(), P()),
        check_vma=False,
    )
```
